256 devices in a mesh: grp: 8 (over x, core), own: 32 (over z, y).
Axes of the slice: x: 4, y: 4, z: 8, core: 2. Of those that a mesh axis runs over, the one named last changes fastest.
Arguments:
- parcels: float32 [1048576, 128], P(('grp', 'own')), may hold values from 0 to 2
- growth_rate: float32 [1048576], P(('grp', 'own')), may hold values from 0.05 to 0.6
- cell_index: int32 [1048576], P(('grp', 'own')), may hold values from 0 to 131071
- dest_owner: int32 [1048576], P(('grp', 'own')), may hold values from 0 to 31, as said below
- live_count: int32 [256], P(('grp', 'own')), may hold values from 2048 to 4096, as said below
- supersat: float32 [4096, 8192], P('grp', 'own'), may hold values from 0.2 to 1.5
- bin_volume: float32 [128], replicated, may hold values from 0.01 to 1
Outputs:
- grown: float32 [2097152, 128], P(('grp', 'own'))
- field: float32 [4096, 8192], P('grp', 'own')
The draws below stay inside these ranges and needn't reach their ends.
Inputs may be any that keep to these rules, and one draw needn't show every extreme that they name: `dest_owner`: among the live rows of one device, at most 256 name any one owner, and some owner is named by exactly 256 of them. `live_count`: some device has all 4096 rows live.
All inputs are finite; a program needn't handle non-finite values.
Results may differ from the reference program's by a relative error of at most 0.0003.
Values sent between devices are 32-bit elements; how exact they have to be, the bound alone decides.
No kernel may reach another device: no remote copies, remote signals or barrier semaphores. Data moves between devices by JAX's collectives and lax.ppermute only.
A program may use at most 64 MiB of HBM per device.

```python
import math
import jax
import jax.numpy as jnp
from jax import lax

BINS = 128
P_DEV = 4096
CZ = 512
CX = 256
ITERS = 4
CAP = 256
SLOTS = 8192
NPAR = 1048576
NZ = 4096
NX = 8192
N_GRP = 8
N_OWN = 32


def live_counts(key):
    devices = NPAR // P_DEV
    counts = jax.random.randint(jax.random.fold_in(key, 11), (devices,), P_DEV // 2, P_DEV + 1)
    full_index = jax.random.randint(jax.random.fold_in(key, 12), (), 0, devices)
    return counts.at[full_index].set(P_DEV).astype(jnp.int32)


def draw_live_count(key, part):
    counts = live_counts(key)
    return counts


def draw_dest_owner(key, part):
    counts = live_counts(key)
    key = jax.random.fold_in(key, 5)
    devices = NPAR // P_DEV
    key_noise, key_base, key_junk = jax.random.split(key, 3)
    row_ids = jnp.arange(P_DEV, dtype=jnp.int32)
    noise = jax.random.randint(key_noise, (devices, P_DEV), 0, 65536)
    alive_rows = row_ids[None, :] < counts[:, None]
    scores = jnp.where(alive_rows, noise * P_DEV + row_ids[None, :], 1073741824 + row_ids[None, :])
    order = jnp.argsort(scores, axis=1, stable=True)
    ranks = jnp.argsort(order, axis=1, stable=True).astype(jnp.int32)
    base_owner = jax.random.randint(key_base, (devices, 1), 0, N_OWN)
    live_dest = (base_owner + ranks // CAP) % N_OWN
    junk_dest = jax.random.randint(key_junk, (devices, P_DEV), 0, N_OWN)
    return jnp.where(alive_rows, live_dest, junk_dest).reshape(-1).astype(jnp.int32)


def plant(values, rng, least, top_value):
    longest = values.shape.index(max(values.shape))
    spots = []
    for shift in (0, 1):
        where = [jax.random.randint(jax.random.fold_in(rng, axis), (), 0, length) for axis, length in enumerate(values.shape)]
        where[longest] = (where[longest] + shift) % values.shape[longest]
        spots.append(tuple(where))
    return values.at[spots[0]].set(least).at[spots[1]].set(top_value)


def level_of(key, shape, pieces, smallest, largest):
    loudness = 1.0
    for dim, shards_of in pieces:
        heights = jax.random.uniform(jax.random.fold_in(jax.random.fold_in(key, 6), dim), (shards_of,), jnp.float32, smallest / len(pieces), largest / len(pieces))
        loudness = loudness * jnp.repeat(jnp.exp(heights), shape[dim] // shards_of).reshape((-1,) + (1,) * (len(shape) - 1 - dim))
    return loudness


def setup_inputs(seed: int = 0) -> dict:
    key_list = jax.random.split(jax.random.key(seed), 8)
    parcels = jnp.clip(2.0 * jax.random.uniform(key_list[0], (NPAR, BINS), jnp.float32) ** level_of(key_list[0], (NPAR, BINS), ((0, 256),), -0.2, 0.2), 0.0, 2.0)
    growth_rate = jnp.clip(jnp.exp(math.log(0.6) - 2.4849067 * jax.random.uniform(key_list[1], (NPAR,), jnp.float32) ** level_of(key_list[1], (NPAR,), ((0, 256),), -0.2, 0.2)), 0.05, 0.6)
    cell_index = plant(jax.random.randint(key_list[2], (NPAR,), 0, CZ * CX), jax.random.fold_in(key_list[2], 1), 0, (CZ * CX) - 1).astype(jnp.int32)
    dest_owner = draw_dest_owner(jax.random.fold_in(key_list[7], 71), 0)
    live_count = draw_live_count(jax.random.fold_in(key_list[7], 71), 0)
    supersat = jnp.clip(0.2 + 1.3 * jax.random.uniform(key_list[5], (NZ, NX), jnp.float32) ** level_of(key_list[5], (NZ, NX), ((0, 8), (1, 32)), -0.2, 0.2), 0.2, 1.5)
    bin_volume = jnp.clip(jnp.exp(jax.random.uniform(key_list[6], (BINS,), jnp.float32, math.log(0.01), math.log(1.0))), 0.01, 1.0)
    return dict(parcels=parcels, growth_rate=growth_rate, cell_index=cell_index, dest_owner=dest_owner, live_count=live_count, supersat=supersat, bin_volume=bin_volume)


def pack_rows(rows, rates, cells, target, count, owners, capacity):
    total_rows = rows.shape[0]
    alive_rows = jnp.arange(total_rows) < count
    hits_dest = (target[:, None] == jnp.arange(owners)[None, :]) & alive_rows[:, None]
    before = jnp.cumsum(hits_dest.astype(jnp.int32), axis=0) - 1
    order_rank = jnp.sum(jnp.where(hits_dest, before, 0), axis=1)
    total_slots = owners * capacity
    slot_pos = jnp.where(alive_rows, target * capacity + order_rank, total_slots)
    slot_rows = jnp.zeros((total_slots, rows.shape[1]), jnp.float32).at[slot_pos].set(rows, mode="drop")
    slot_rates = jnp.zeros((total_slots,), jnp.float32).at[slot_pos].set(rates, mode="drop")
    slot_cells = jnp.full((total_slots,), -1, jnp.int32).at[slot_pos].set(cells.astype(jnp.int32), mode="drop")
    return slot_rows, slot_rates, slot_cells


def smooth_field(field):
    padded = jnp.pad(field, 1)
    beside_all = padded[2:, 1:-1] + padded[:-2, 1:-1] + padded[1:-1, 2:] + padded[1:-1, :-2]
    return field + 0.2 * (beside_all - 4.0 * field)


def reference(parcels, growth_rate, cell_index, dest_owner, live_count, supersat, bin_volume):
    groups = N_GRP
    owners = N_OWN
    devices = groups * owners

    def pack_one(items):
        return pack_rows(items[0], items[1], items[2], items[3], items[4], owners, CAP)

    slot_rows, slot_rates, slot_cells = lax.map(pack_one, (parcels.reshape(devices, P_DEV, BINS), growth_rate.reshape(devices, P_DEV), cell_index.reshape(devices, P_DEV), dest_owner.reshape(devices, P_DEV), live_count))
    slot_rows = slot_rows.reshape(groups, owners, owners, CAP, BINS).transpose(0, 2, 1, 3, 4).reshape(devices, SLOTS, BINS)
    slot_rates = slot_rates.reshape(groups, owners, owners, CAP).transpose(0, 2, 1, 3).reshape(devices, SLOTS)
    slot_cells = slot_cells.reshape(groups, owners, owners, CAP).transpose(0, 2, 1, 3).reshape(devices, SLOTS)
    local_fields = supersat.reshape(groups, CZ, owners, CX).transpose(0, 2, 1, 3).reshape(devices, CZ * CX)

    def grow_one(items):
        rows, rates, cells, flat_field = items
        valid = cells >= 0
        safe_cells = jnp.where(valid, cells, 0)
        saturation = jnp.where(valid, flat_field[safe_cells], jnp.float32(0.0))
        courant = rates * saturation
        previous = jnp.pad(rows[:, :-1], ((0, 0), (1, 0)))
        diff = rows - previous
        new_rows = rows - courant[:, None] * diff
        mass = courant * jnp.sum(diff * bin_volume[None, :], axis=1)
        source = jnp.zeros((CZ * CX,), jnp.float32).at[jnp.where(valid, cells, CZ * CX)].add(mass, mode="drop")
        return new_rows, source

    grown, source = lax.map(grow_one, (slot_rows, slot_rates, slot_cells, local_fields))
    source = source.reshape(groups, owners, CZ, CX).transpose(0, 2, 1, 3).reshape(NZ, NX)
    field = supersat - 0.5 * source
    for sweep in range(ITERS):
        field = smooth_field(field)
    return grown.reshape(devices * SLOTS, BINS), field
```

```python
import functools

import jax
import jax.numpy as jnp
from jax import lax
from jax.experimental import pallas as pl
from jax.experimental.pallas import tpu as pltpu
from jax.sharding import PartitionSpec as P

ITERS = 4
LANES = 128
FIRST = 32
META = 8
NT = (((1,), (1,)), ((), ()))
NN = (((1,), (0,)), ((), ()))
VMEM_LIMIT = 40 * 1024 * 1024


def dot(a, b, dims):
    return lax.dot_general(a, b, dims, preferred_element_type=jnp.float32)


def split3(x):
    hi = x.astype(jnp.bfloat16).astype(jnp.float32)
    rest = x - hi
    mid = rest.astype(jnp.bfloat16).astype(jnp.float32)
    return hi, mid, rest - mid


def iota(shape, dim):
    return lax.broadcasted_iota(jnp.int32, shape, dim)


def params(**kw):
    return pltpu.CompilerParams(vmem_limit_bytes=VMEM_LIMIT, **kw)


def plan_kernel(
    live_ref, dest_ref, rate_ref, cell_ref, vol_ref, rows_hbm,
    first_ref, src_ref,
    rows_v, lhs, bt, vrow, src_smem, sem_rows, sem_src,
):
    chunks = dest_ref.shape[0]
    owners, cap = src_ref.shape
    total = chunks * LANES
    load = pltpu.make_async_copy(rows_hbm, rows_v.at[pl.ds(0, total)], sem_rows)
    load.start()
    rows_v[total : total + 8, :] = jnp.zeros((8, LANES), jnp.float32)

    live = live_ref[0]
    lane = iota((1, LANES), 1)
    owner_of = iota((owners, LANES), 0)
    tri = (iota((LANES, 2 * LANES), 0) <= iota((LANES, 2 * LANES), 1)).astype(jnp.bfloat16)
    hits = []
    for s in range(chunks):
        target = jnp.where(lane + s * LANES < live, dest_ref[s : s + 1, :], -1)
        hits.append((owner_of == target).astype(jnp.float32))
    counts = dot(jnp.concatenate(hits, axis=0).astype(jnp.bfloat16), tri, NN)

    load.wait()
    vol = vol_ref[...]
    shifted = jnp.where(lane == LANES - 1, 0.0, pltpu.roll(vol, LANES - 1, 1))
    w_hi, w_mid, w_lo = split3(vol - shifted)
    weights = jnp.concatenate(
        [w_hi, w_mid, w_lo, jnp.zeros((5, LANES), jnp.float32)], axis=0
    ).astype(jnp.bfloat16)
    span = 512
    for s in range(total // span):
        r_hi, r_mid, r_lo = split3(rows_v[s * span : (s + 1) * span, :])
        p_hi = dot(weights, r_hi.astype(jnp.bfloat16), NT)
        p_mid = dot(weights, r_mid.astype(jnp.bfloat16), NT)
        p_lo = dot(weights, r_lo.astype(jnp.bfloat16), NT)
        v = p_hi[0:1] + (p_hi[1:2] + p_mid[0:1]) + (p_hi[2:3] + p_mid[1:2] + p_lo[0:1])
        vrow[:, s * span : (s + 1) * span] = v

    rank_of = iota((cap, LANES), 0).astype(jnp.float32)
    carry = jnp.zeros((owners, LANES), jnp.float32)
    for s in range(chunks):
        hit = hits[s]
        part = counts[s * owners : (s + 1) * owners]
        rank = jnp.sum(hit * (part[:, :LANES] + carry - 1.0), axis=0, keepdims=True)
        carry = carry + part[:, LANES:]
        cols = slice(s * LANES, (s + 1) * LANES)
        bt[:, cols] = (rank_of == rank).astype(jnp.float32).astype(jnp.bfloat16)
        cell = cell_ref[s : s + 1, :]
        cell_hi = jnp.right_shift(cell + 256, 9)
        cell_lo = cell - cell_hi * 512
        values = (
            (jnp.full((1, LANES), s + 1, jnp.float32), lane.astype(jnp.float32))
            + split3(rate_ref[s : s + 1, :])
            + (cell_hi.astype(jnp.float32), cell_lo.astype(jnp.float32))
            + split3(vrow[:, cols])
        )
        for q, value in enumerate(values):
            lhs[q * owners : (q + 1) * owners, cols] = (hit * value).astype(jnp.bfloat16)

    packed = dot(lhs[...], bt[...], NT)
    part = [packed[q * owners : (q + 1) * owners] for q in range(10)]
    src = jnp.where(part[0] > 0.5, (part[0] - 1.0) * LANES + part[1], float(total))
    src_ref[...] = src.astype(jnp.int32)
    to_smem = pltpu.make_async_copy(src_ref, src_smem, sem_src)
    to_smem.start()
    meta = (
        part[2] + part[3] + part[4],
        part[5] * 512.0 + part[6],
        part[7] + part[8] + part[9],
    )
    first = first_ref.shape[1] - META
    for q, value in enumerate(meta):
        for half in range(2):
            at = first + 2 * q + half
            for j in range(owners):
                first_ref[j, at : at + 1, :] = value[j : j + 1, half * LANES : (half + 1) * LANES]
    for j in range(owners):
        first_ref[j, first + 6 : first + 8, :] = jnp.zeros((2, LANES), jnp.float32)
    to_smem.wait()

    def copy_rows(j, _):
        for r in range(first):
            first_ref[j, r : r + 1, :] = rows_v[pl.ds(src_smem[j, r], 1), :]
        return 0

    lax.fori_loop(0, owners, copy_rows, 0)


def plan(live, dest, rate, cell, vol, rows, owners, cap):
    chunks = dest.shape[0]
    total = chunks * LANES
    vm = pl.BlockSpec(memory_space=pltpu.VMEM)
    return pl.pallas_call(
        plan_kernel,
        in_specs=[pl.BlockSpec(memory_space=pltpu.SMEM), vm, vm, vm, vm, pl.BlockSpec(memory_space=pl.ANY)],
        out_specs=(vm, vm),
        out_shape=(
            jax.ShapeDtypeStruct((owners, FIRST + META, LANES), jnp.float32),
            jax.ShapeDtypeStruct((owners, cap), jnp.int32),
        ),
        scratch_shapes=[
            pltpu.VMEM((total + 8, LANES), jnp.float32),
            pltpu.VMEM((10 * owners, total), jnp.bfloat16),
            pltpu.VMEM((cap, total), jnp.bfloat16),
            pltpu.VMEM((1, total), jnp.float32),
            pltpu.SMEM((owners, cap), jnp.int32),
            pltpu.SemaphoreType.DMA,
            pltpu.SemaphoreType.DMA,
        ],
        compiler_params=params(),
        name="plan",
    )(live, dest, rate, cell, vol, rows)


def pack_kernel(src_ref, rows_hbm, out_ref, rows_v, sem):
    total = rows_v.shape[0] - 8
    per_step, ranks, _ = out_ref.shape
    step = pl.program_id(0)

    @pl.when(step == 0)
    def _():
        load = pltpu.make_async_copy(rows_hbm, rows_v.at[pl.ds(0, total)], sem)
        load.start()
        rows_v[total : total + 8, :] = jnp.zeros((8, LANES), jnp.float32)
        load.wait()

    def copy_rows(i, _):
        j = i // (ranks // 32)
        base = (i % (ranks // 32)) * 32
        for r in range(32):
            at = src_ref[step * per_step + j, FIRST + base + r]
            out_ref[j, pl.ds(base + r, 1), :] = rows_v[pl.ds(at, 1), :]
        return 0

    lax.fori_loop(0, per_step * (ranks // 32), copy_rows, 0)


def pack(src, rows):
    owners, cap = src.shape
    total = rows.shape[0]
    per_step = 8
    ranks = cap - FIRST
    return pl.pallas_call(
        pack_kernel,
        grid=(owners // per_step,),
        in_specs=[pl.BlockSpec(memory_space=pltpu.SMEM), pl.BlockSpec(memory_space=pl.ANY)],
        out_specs=pl.BlockSpec((per_step, ranks, LANES), lambda i: (i, 0, 0)),
        out_shape=jax.ShapeDtypeStruct((owners, ranks, LANES), jnp.float32),
        scratch_shapes=[pltpu.VMEM((total + 8, LANES), jnp.float32), pltpu.SemaphoreType.DMA],
        compiler_params=params(),
        cost_estimate=pl.CostEstimate(flops=0, bytes_accessed=24 << 20, transcendentals=0),
        name="pack",
    )(src, rows)


def deposit_kernel(
    meta_ref, sup_ref, field_ref, cour_ref, top_ref, bottom_ref, left_ref, right_ref,
    table, high, acc, cour,
):
    depth, width = sup_ref.shape
    owners = meta_ref.shape[0]
    group = 4
    n = group * 2 * LANES
    flipped = jnp.transpose(sup_ref[...])
    f_hi = flipped.astype(jnp.bfloat16)
    table[:width, :] = f_hi
    table[width:, :] = (flipped - f_hi.astype(jnp.float32)).astype(jnp.bfloat16)
    acc[...] = jnp.zeros_like(acc)

    def step(g, _):
        def lane_row(q):
            return jnp.concatenate(
                [meta_ref[g * group + o, 2 * q + half : 2 * q + half + 1, :] for o in range(group) for half in range(2)],
                axis=1,
            )

        rate, cell, v = lane_row(0), lane_row(1).astype(jnp.int32), lane_row(2)
        row_at = jnp.right_shift(cell, 8)
        col_at = jnp.bitwise_and(cell, 255)
        high[...] = (iota((depth, n), 0) == row_at).astype(jnp.float32).astype(jnp.bfloat16)
        lines = dot(table[...], high[...], NN)
        across = iota((width, n), 0) == col_at
        sat = jnp.sum(jnp.where(across, lines[:width] + lines[width:], 0.0), axis=0, keepdims=True)
        courant = rate * sat
        for o in range(group):
            cour[pl.ds(g * group + o, 1), :] = courant[:, o * 2 * LANES : (o + 1) * 2 * LANES]
        mass = courant * v
        m_hi = mass.astype(jnp.bfloat16).astype(jnp.float32)
        spread = jnp.concatenate(
            [jnp.where(across, m_hi, 0.0).astype(jnp.bfloat16), jnp.where(across, mass - m_hi, 0.0).astype(jnp.bfloat16)],
            axis=0,
        )
        acc[...] += dot(high[...], spread, NT)
        return 0

    lax.fori_loop(0, owners // group, step, 0)
    field = sup_ref[...] - 0.5 * (acc[:, :width] + acc[:, width:])
    field_ref[...] = field
    cour_ref[...] = jnp.transpose(cour[...])
    top_ref[...] = field[:8]
    bottom_ref[...] = field[depth - 8 :]
    left_ref[...] = jnp.transpose(field[:, :LANES])[:8]
    right_ref[...] = jnp.transpose(field[:, width - LANES :])[LANES - 8 :]


def deposit(got_first, supersat):
    owners = got_first.shape[0]
    depth, width = supersat.shape
    f32 = jnp.float32
    full = lambda shape: pl.BlockSpec(shape, lambda i: (0,) * len(shape))
    outs = [(depth, width), (2 * LANES, owners), (8, width), (8, width), (8, depth), (8, depth)]
    return pl.pallas_call(
        deposit_kernel,
        grid=(1,),
        in_specs=[
            pl.BlockSpec((owners, META, LANES), lambda i: (0, FIRST // META, 0)),
            full((depth, width)),
        ],
        out_specs=[full(s) for s in outs],
        out_shape=[jax.ShapeDtypeStruct(s, f32) for s in outs],
        scratch_shapes=[
            pltpu.VMEM((2 * width, depth), jnp.bfloat16),
            pltpu.VMEM((depth, 8 * LANES), jnp.bfloat16),
            pltpu.VMEM((depth, 2 * width), f32),
            pltpu.VMEM((owners, 2 * LANES), f32),
        ],
        compiler_params=params(),
        cost_estimate=pl.CostEstimate(flops=9 << 30, bytes_accessed=8 << 20, transcendentals=0),
        name="deposit",
    )(got_first, supersat)


def side_lanes(cols, low):
    rows = cols.shape[1]
    zeros = jnp.zeros((LANES - 8, rows), jnp.float32)
    return jnp.transpose(jnp.concatenate([zeros, cols] if low else [cols, zeros], axis=0))


def corners_kernel(top_ref, bottom_ref, left_ref, right_ref, out_top, out_bottom):
    depth = left_ref.shape[1]
    left = side_lanes(left_ref[...], True)
    right = side_lanes(right_ref[...], False)
    out_top[...] = jnp.concatenate([left[:8], top_ref[...], right[:8]], axis=1)
    out_bottom[...] = jnp.concatenate([left[depth - 8 :], bottom_ref[...], right[depth - 8 :]], axis=1)


def corners(top, bottom, left, right):
    wide = top.shape[1] + 2 * LANES
    return pl.pallas_call(
        corners_kernel,
        out_shape=[jax.ShapeDtypeStruct((8, wide), jnp.float32)] * 2,
        compiler_params=params(),
        name="corners",
    )(top, bottom, left, right)


def smooth_kernel(edge_ref, field_ref, left_ref, right_ref, up_ref, down_ref, out_ref):
    depth, width = field_ref.shape
    middle = jnp.concatenate(
        [side_lanes(left_ref[...], True), field_ref[...], side_lanes(right_ref[...], False)], axis=1
    )
    x = jnp.concatenate([up_ref[...], middle, down_ref[...]], axis=0)
    tall, wide = x.shape
    row, col = iota(x.shape, 0), iota(x.shape, 1)
    row_lo = jnp.where(edge_ref[0] == 0, 8, 0)
    row_hi = jnp.where(edge_ref[0] == edge_ref[2] - 1, 8 + depth, tall)
    col_lo = jnp.where(edge_ref[1] == 0, LANES, 0)
    col_hi = jnp.where(edge_ref[1] == edge_ref[3] - 1, LANES + width, wide)
    inside = (row >= row_lo) & (row < row_hi) & (col >= col_lo) & (col < col_hi)
    for _ in range(ITERS):
        beside = pltpu.roll(x, tall - 1, 0) + pltpu.roll(x, 1, 0) + pltpu.roll(x, wide - 1, 1) + pltpu.roll(x, 1, 1)
        x = jnp.where(inside, x + 0.2 * (beside - 4.0 * x), 0.0)
    out_ref[...] = x[8 : 8 + depth, LANES : LANES + width]


def smooth(edge, field, left, right, up, down):
    vm = pl.BlockSpec(memory_space=pltpu.VMEM)
    return pl.pallas_call(
        smooth_kernel,
        in_specs=[pl.BlockSpec(memory_space=pltpu.SMEM)] + [vm] * 5,
        out_specs=vm,
        out_shape=jax.ShapeDtypeStruct(field.shape, jnp.float32),
        compiler_params=params(),
        name="smooth",
    )(edge, field, left, right, up, down)


def grow_kernel(rows_ref, cour_ref, *rest):
    out_ref = rest[-1]
    owners, ranks, _ = rows_ref.shape
    keep = iota((ranks, LANES), 1) > 0
    for o in range(owners):
        x = rows_ref[o]
        before = jnp.where(keep, pltpu.roll(x, 1, 1), 0.0)
        out_ref[o] = x - cour_ref[:, o : o + 1] * (x - before)


def grow(rows, cour, begin, steps, onto=None):
    cap, owners = cour.shape
    block = (owners, FIRST, LANES)
    operands = [rows, cour]
    in_specs = [
        pl.BlockSpec(block, lambda k: (0, k, 0)),
        pl.BlockSpec((FIRST, owners), lambda k: (k + begin, 0)),
    ]
    aliases = {}
    if onto is not None:
        operands.append(onto)
        in_specs.append(pl.BlockSpec(memory_space=pl.ANY))
        aliases = {2: 0}
    return pl.pallas_call(
        grow_kernel,
        grid=(steps,),
        in_specs=in_specs,
        out_specs=pl.BlockSpec(block, lambda k: (0, k + begin, 0)),
        out_shape=jax.ShapeDtypeStruct((owners, cap, LANES), jnp.float32),
        input_output_aliases=aliases,
        compiler_params=params(),
        name="grow",
    )(*operands)


def neighbours(low_part, high_part, axis):
    count = lax.axis_size(axis)
    forward = [(i, i + 1) for i in range(count - 1)]
    backward = [(i + 1, i) for i in range(count - 1)]
    return lax.ppermute(high_part, axis, forward), lax.ppermute(low_part, axis, backward)


def per_device(parcels, growth_rate, cell_index, dest_owner, live_count, supersat, bin_volume):
    owners = lax.axis_size("own")
    total = parcels.shape[0]
    cap = 2 * total // owners
    chunks = total // LANES
    square = lambda x: x.reshape(chunks, LANES)
    exchange = functools.partial(lax.all_to_all, axis_name="own", split_axis=0, concat_axis=0, tiled=True)
    first, src = plan(
        live_count, square(dest_owner), square(growth_rate), square(cell_index), bin_volume.reshape(1, LANES), parcels, owners, cap
    )
    got_first = exchange(first)
    rest = pack(src, parcels)
    got_rest = exchange(rest)

    field, cour, top, bottom, left, right = deposit(got_first, supersat)
    got_left, got_right = neighbours(left, right, "own")
    ext_top, ext_bottom = corners(top, bottom, got_left, got_right)
    got_up, got_down = neighbours(ext_top, ext_bottom, "grp")
    edge = jnp.stack([lax.axis_index("grp"), lax.axis_index("own"), lax.axis_size("grp"), owners]).astype(jnp.int32)
    field = smooth(edge, field, got_left, got_right, got_up, got_down)

    grown = grow(got_first, cour, 0, 1)
    grown = grow(got_rest, cour, 1, cap // FIRST - 1, grown)
    return grown.reshape(owners * cap, LANES), field


def solution(mesh):
    placed = (
        P(("grp", "own"), None),
        P(("grp", "own")),
        P(("grp", "own")),
        P(("grp", "own")),
        P(("grp", "own")),
        P("grp", "own"),
        P(),
    )
    return jax.shard_map(
        per_device,
        mesh=mesh,
        in_specs=placed,
        out_specs=(P(("grp", "own"), None), P("grp", "own")),
        check_vma=False,
    )
```

```python
import functools

import jax
import jax.numpy as jnp
from jax import lax
from jax.experimental import pallas as pl
from jax.experimental.pallas import tpu as pltpu
from jax.sharding import PartitionSpec as P

ITERS = 4
LANES = 128
FIRST = 32
META = 8
NT = (((1,), (1,)), ((), ()))
NN = (((1,), (0,)), ((), ()))
VMEM_LIMIT = 56 * 1024 * 1024
PARTS = 8


def dot(a, b, dims):
    return lax.dot_general(a, b, dims, preferred_element_type=jnp.float32)


def split3(x):
    hi = x.astype(jnp.bfloat16).astype(jnp.float32)
    rest = x - hi
    mid = rest.astype(jnp.bfloat16).astype(jnp.float32)
    return hi, mid, rest - mid


def iota(shape, dim):
    return lax.broadcasted_iota(jnp.int32, shape, dim)


def params(**kw):
    return pltpu.CompilerParams(vmem_limit_bytes=VMEM_LIMIT, **kw)


def copies(pairs, sems):
    return [pltpu.make_async_copy(a, b, sems.at[i]) for i, (a, b) in enumerate(pairs)]


def plan_kernel(
    live_ref, dest_hbm, rate_hbm, cell_hbm, vol_hbm, rows_hbm,
    first_hbm, src_ref,
    dest_ref, rate_ref, cell_ref, vol_ref, rows_v, first_ref, lhs, bt, vrow, src_smem, sem_in, sem_src, sem_out,
):
    chunks = dest_ref.shape[0]
    owners, cap = src_ref.shape
    total = chunks * LANES
    loads = copies(
        [
            (dest_hbm, dest_ref),
            (rows_hbm, rows_v.at[pl.ds(0, total)]),
            (vol_hbm, vol_ref),
            (rate_hbm, rate_ref),
            (cell_hbm, cell_ref),
        ],
        sem_in,
    )
    for c in loads:
        c.start()
    rows_v[total : total + 8, :] = jnp.zeros((8, LANES), jnp.float32)
    loads[0].wait()

    live = live_ref[0]
    lane = iota((1, LANES), 1)
    owner_of = iota((owners, LANES), 0)
    tri = (iota((LANES, 2 * LANES), 0) <= iota((LANES, 2 * LANES), 1)).astype(jnp.bfloat16)
    hits = []
    for s in range(chunks):
        target = jnp.where(lane + s * LANES < live, dest_ref[s : s + 1, :], -1)
        hits.append((owner_of == target).astype(jnp.float32))
    counts = dot(jnp.concatenate(hits, axis=0).astype(jnp.bfloat16), tri, NN)

    for c in loads[1:]:
        c.wait()
    vol = vol_ref[...]
    shifted = jnp.where(lane == LANES - 1, 0.0, pltpu.roll(vol, LANES - 1, 1))
    w_hi, w_mid, w_lo = split3(vol - shifted)
    weights = jnp.concatenate(
        [w_hi, w_mid, w_lo, jnp.zeros((5, LANES), jnp.float32)], axis=0
    ).astype(jnp.bfloat16)
    span = 512
    for s in range(total // span):
        r_hi, r_mid, r_lo = split3(rows_v[s * span : (s + 1) * span, :])
        p_hi = dot(weights, r_hi.astype(jnp.bfloat16), NT)
        p_mid = dot(weights, r_mid.astype(jnp.bfloat16), NT)
        p_lo = dot(weights, r_lo.astype(jnp.bfloat16), NT)
        v = p_hi[0:1] + (p_hi[1:2] + p_mid[0:1]) + (p_hi[2:3] + p_mid[1:2] + p_lo[0:1])
        vrow[:, s * span : (s + 1) * span] = v

    rank_of = iota((cap, LANES), 0).astype(jnp.float32)
    carry = jnp.zeros((owners, LANES), jnp.float32)
    for s in range(chunks):
        hit = hits[s]
        part = counts[s * owners : (s + 1) * owners]
        rank = jnp.sum(hit * (part[:, :LANES] + carry - 1.0), axis=0, keepdims=True)
        carry = carry + part[:, LANES:]
        cols = slice(s * LANES, (s + 1) * LANES)
        bt[:, cols] = (rank_of == rank).astype(jnp.float32).astype(jnp.bfloat16)
        cell = cell_ref[s : s + 1, :]
        cell_hi = jnp.right_shift(cell + 256, 9)
        cell_lo = cell - cell_hi * 512
        values = (
            (jnp.full((1, LANES), s + 1, jnp.float32), lane.astype(jnp.float32))
            + split3(rate_ref[s : s + 1, :])
            + (cell_hi.astype(jnp.float32), cell_lo.astype(jnp.float32))
            + split3(vrow[:, cols])
        )
        for q, value in enumerate(values):
            lhs[q * owners : (q + 1) * owners, cols] = (hit * value).astype(jnp.bfloat16)

    packed = dot(lhs[...], bt[...], NT)
    part = [packed[q * owners : (q + 1) * owners] for q in range(10)]
    src = jnp.where(part[0] > 0.5, (part[0] - 1.0) * LANES + part[1], float(total))
    src_ref[...] = src.astype(jnp.int32)
    to_smem = pltpu.make_async_copy(src_ref, src_smem, sem_src)
    to_smem.start()
    meta = (
        part[2] + part[3] + part[4],
        part[5] * 512.0 + part[6],
        part[7] + part[8] + part[9],
    )
    first = first_ref.shape[1] - META
    for q, value in enumerate(meta):
        for half in range(2):
            at = first + 2 * q + half
            for j in range(owners):
                first_ref[j, at : at + 1, :] = value[j : j + 1, half * LANES : (half + 1) * LANES]
    for j in range(owners):
        first_ref[j, first + 6 : first + 8, :] = jnp.zeros((2, LANES), jnp.float32)
    to_smem.wait()

    def copy_rows(j, _):
        at = [src_smem[j, r] for r in range(first)]
        rows = [rows_v[pl.ds(i, 1), :] for i in at]
        for r in range(first):
            first_ref[j, r : r + 1, :] = rows[r]
        return 0

    lax.fori_loop(0, owners, copy_rows, 0)
    store = pltpu.make_async_copy(first_ref, first_hbm, sem_out)
    store.start()
    store.wait()


def plan(live, dest, rate, cell, vol, rows, owners, cap):
    chunks = dest.shape[0]
    total = chunks * LANES
    hbm = pl.BlockSpec(memory_space=pltpu.HBM)
    return pl.pallas_call(
        plan_kernel,
        in_specs=[pl.BlockSpec(memory_space=pltpu.SMEM)] + [hbm] * 5,
        out_specs=(hbm, pl.BlockSpec(memory_space=pltpu.VMEM)),
        out_shape=(
            jax.ShapeDtypeStruct((owners, FIRST + META, LANES), jnp.float32),
            jax.ShapeDtypeStruct((owners, cap), jnp.int32),
        ),
        scratch_shapes=[
            pltpu.VMEM((chunks, LANES), jnp.int32),
            pltpu.VMEM((chunks, LANES), jnp.float32),
            pltpu.VMEM((chunks, LANES), jnp.int32),
            pltpu.VMEM((1, LANES), jnp.float32),
            pltpu.VMEM((total + 8, LANES), jnp.float32),
            pltpu.VMEM((owners, FIRST + META, LANES), jnp.float32),
            pltpu.VMEM((10 * owners, total), jnp.bfloat16),
            pltpu.VMEM((cap, total), jnp.bfloat16),
            pltpu.VMEM((1, total), jnp.float32),
            pltpu.SMEM((owners, cap), jnp.int32),
            pltpu.SemaphoreType.DMA((5,)),
            pltpu.SemaphoreType.DMA,
            pltpu.SemaphoreType.DMA,
        ],
        compiler_params=params(),
        name="plan",
    )(live, dest, rate, cell, vol, rows)


def pack_kernel(src_ref, rows_hbm, out_hbm, rows_v, out_v, sem_rows, sem_out):
    total = rows_v.shape[0] - 8
    owners, ranks, _ = out_v.shape
    load = pltpu.make_async_copy(rows_hbm, rows_v.at[pl.ds(0, total)], sem_rows)
    load.start()
    rows_v[total : total + 8, :] = jnp.zeros((8, LANES), jnp.float32)
    load.wait()
    per = owners // PARTS
    spans = [pl.ds(i * per, per) for i in range(PARTS)]
    stores = copies([(out_v.at[s], out_hbm.at[s]) for s in spans], sem_out)

    def copy_rows(j, _):
        for base in range(0, ranks, 32):
            at = [src_ref[j, FIRST + base + r] for r in range(32)]
            rows = [rows_v[pl.ds(i, 1), :] for i in at]
            for r in range(32):
                out_v[j, base + r : base + r + 1, :] = rows[r]
        return 0

    for i in range(PARTS):
        lax.fori_loop(i * per, (i + 1) * per, copy_rows, 0)
        stores[i].start()
    for c in stores:
        c.wait()


def pack(src, rows):
    owners, cap = src.shape
    total = rows.shape[0]
    hbm = pl.BlockSpec(memory_space=pltpu.HBM)
    shape = (owners, cap - FIRST, LANES)
    return pl.pallas_call(
        pack_kernel,
        in_specs=[pl.BlockSpec(memory_space=pltpu.SMEM), hbm],
        out_specs=hbm,
        out_shape=jax.ShapeDtypeStruct(shape, jnp.float32),
        scratch_shapes=[
            pltpu.VMEM((total + 8, LANES), jnp.float32),
            pltpu.VMEM(shape, jnp.float32),
            pltpu.SemaphoreType.DMA,
            pltpu.SemaphoreType.DMA((PARTS,)),
        ],
        compiler_params=params(),
        cost_estimate=pl.CostEstimate(flops=0, bytes_accessed=24 << 20, transcendentals=0),
        name="pack",
    )(src, rows)


def deposit_kernel(
    meta_ref, sup_ref, field_ref, cour_ref, top_ref, bottom_ref, left_ref, right_ref,
    table, high, acc, cour,
):
    depth, width = sup_ref.shape
    owners = meta_ref.shape[0]
    group = 4
    n = group * 2 * LANES
    flipped = jnp.transpose(sup_ref[...])
    f_hi = flipped.astype(jnp.bfloat16)
    table[:width, :] = f_hi
    table[width:, :] = (flipped - f_hi.astype(jnp.float32)).astype(jnp.bfloat16)
    acc[...] = jnp.zeros_like(acc)

    def step(g, _):
        def lane_row(q):
            return jnp.concatenate(
                [meta_ref[g * group + o, 2 * q + half : 2 * q + half + 1, :] for o in range(group) for half in range(2)],
                axis=1,
            )

        rate, cell, v = lane_row(0), lane_row(1).astype(jnp.int32), lane_row(2)
        row_at = jnp.right_shift(cell, 8)
        col_at = jnp.bitwise_and(cell, 255)
        high[...] = (iota((depth, n), 0) == row_at).astype(jnp.float32).astype(jnp.bfloat16)
        lines = dot(table[...], high[...], NN)
        across = iota((width, n), 0) == col_at
        sat = jnp.sum(jnp.where(across, lines[:width] + lines[width:], 0.0), axis=0, keepdims=True)
        courant = rate * sat
        for o in range(group):
            cour[pl.ds(g * group + o, 1), :] = courant[:, o * 2 * LANES : (o + 1) * 2 * LANES]
        mass = courant * v
        m_hi = mass.astype(jnp.bfloat16).astype(jnp.float32)
        spread = jnp.concatenate(
            [jnp.where(across, m_hi, 0.0).astype(jnp.bfloat16), jnp.where(across, mass - m_hi, 0.0).astype(jnp.bfloat16)],
            axis=0,
        )
        acc[...] += dot(high[...], spread, NT)
        return 0

    lax.fori_loop(0, owners // group, step, 0)
    field = sup_ref[...] - 0.5 * (acc[:, :width] + acc[:, width:])
    field_ref[...] = field
    cour_ref[...] = jnp.transpose(cour[...])
    top_ref[...] = field[:8]
    bottom_ref[...] = field[depth - 8 :]
    left_ref[...] = jnp.transpose(field[:, :LANES])[:8]
    right_ref[...] = jnp.transpose(field[:, width - LANES :])[LANES - 8 :]


def deposit(got_first, supersat):
    owners = got_first.shape[0]
    depth, width = supersat.shape
    f32 = jnp.float32
    full = lambda shape: pl.BlockSpec(shape, lambda i: (0,) * len(shape))
    outs = [(depth, width), (2 * LANES, owners), (8, width), (8, width), (8, depth), (8, depth)]
    return pl.pallas_call(
        deposit_kernel,
        grid=(1,),
        in_specs=[
            pl.BlockSpec((owners, META, LANES), lambda i: (0, FIRST // META, 0)),
            full((depth, width)),
        ],
        out_specs=[full(s) for s in outs],
        out_shape=[jax.ShapeDtypeStruct(s, f32) for s in outs],
        scratch_shapes=[
            pltpu.VMEM((2 * width, depth), jnp.bfloat16),
            pltpu.VMEM((depth, 8 * LANES), jnp.bfloat16),
            pltpu.VMEM((depth, 2 * width), f32),
            pltpu.VMEM((owners, 2 * LANES), f32),
        ],
        compiler_params=params(),
        cost_estimate=pl.CostEstimate(flops=9 << 30, bytes_accessed=8 << 20, transcendentals=0),
        name="deposit",
    )(got_first, supersat)


def sides_kernel(up_ref, down_ref, left_ref, right_ref, out_left, out_right):
    depth = left_ref.shape[1]
    width = up_ref.shape[1]
    lane = iota((8, LANES), 1)
    for out, own_ref, begin in ((out_left, left_ref, 0), (out_right, right_ref, width - LANES)):
        skip = 0 if begin == 0 else LANES - 8
        ends = jnp.concatenate([up_ref[:, begin : begin + LANES], down_ref[:, begin : begin + LANES]], axis=0)
        ends = jnp.concatenate([ends, jnp.zeros((LANES - 16, LANES), jnp.float32)], axis=0)
        ends = jnp.transpose(ends)[skip : skip + 8]
        out[:, : depth] = own_ref[...]
        out[:, depth:] = jnp.where(lane < 16, ends, 0.0)


def sides(up, down, left, right):
    shape = (8, left.shape[1] + LANES)
    return pl.pallas_call(
        sides_kernel,
        out_shape=[jax.ShapeDtypeStruct(shape, jnp.float32)] * 2,
        compiler_params=params(),
        name="sides",
    )(up, down, left, right)


def passes(x, inside):
    tall, wide = x.shape
    for _ in range(ITERS):
        beside = pltpu.roll(x, tall - 1, 0) + pltpu.roll(x, 1, 0) + pltpu.roll(x, wide - 1, 1) + pltpu.roll(x, 1, 1)
        x = jnp.where(inside, x + 0.2 * (beside - 4.0 * x), 0.0)
    return x


def smooth_kernel(where_ref, field_ref, up_ref, down_ref, out_ref):
    depth, width = field_ref.shape
    x = jnp.concatenate([up_ref[...], field_ref[...], down_ref[...]], axis=0)
    row = iota(x.shape, 0)
    inside = (row >= jnp.where(where_ref[0] == 0, 8, 0)) & (
        row < jnp.where(where_ref[0] == where_ref[2] - 1, 8 + depth, 16 + depth)
    )
    out_ref[...] = passes(x, inside)[8 : 8 + depth]


def smooth(where, field, up, down):
    vm = pl.BlockSpec(memory_space=pltpu.VMEM)
    return pl.pallas_call(
        smooth_kernel,
        in_specs=[pl.BlockSpec(memory_space=pltpu.SMEM)] + [vm] * 3,
        out_specs=vm,
        out_shape=jax.ShapeDtypeStruct(field.shape, jnp.float32),
        compiler_params=params(),
        name="smooth",
    )(where, field, up, down)


def strip(where_ref, low, high, low_out, high_out):
    depth = low.shape[1] - LANES
    x = jnp.concatenate([low, high], axis=0)
    tail = x[:, depth:]
    lane = iota(tail.shape, 1)
    above = jnp.where(lane >= LANES - 8, pltpu.roll(tail, LANES - 8, 1), 0.0)
    below = jnp.where(lane < 8, pltpu.roll(tail, LANES - 8, 1), 0.0)
    x = jnp.concatenate([above, x[:, :depth], below], axis=1)
    row, col = iota(x.shape, 0), iota(x.shape, 1)
    inside = (
        (row >= jnp.where(low_out, 8, 0))
        & (row < jnp.where(high_out, 8, 16))
        & (col >= jnp.where(where_ref[0] == 0, LANES, 0))
        & (col < jnp.where(where_ref[0] == where_ref[2] - 1, LANES + depth, 2 * LANES + depth))
    )
    return passes(x, inside)[:, LANES : LANES + depth]


def grow_kernel(rows_ref, cour_ref, *rest):
    out_ref = rest[-1]
    owners, ranks, _ = rows_ref.shape
    keep = iota((ranks, LANES), 1) > 0
    for o in range(owners):
        x = rows_ref[o]
        before = jnp.where(keep, pltpu.roll(x, 1, 1), 0.0)
        out_ref[o] = x - cour_ref[:, o : o + 1] * (x - before)


def grow_first(rows, cour):
    cap, owners = cour.shape
    block = (owners, FIRST, LANES)
    return pl.pallas_call(
        grow_kernel,
        grid=(1,),
        in_specs=[pl.BlockSpec(block, lambda k: (0, 0, 0)), pl.BlockSpec((FIRST, owners), lambda k: (0, 0))],
        out_specs=pl.BlockSpec(block, lambda k: (0, 0, 0)),
        out_shape=jax.ShapeDtypeStruct((owners, cap, LANES), jnp.float32),
        compiler_params=params(),
        name="grow_first",
    )(rows, cour)


def finish_kernel(
    where_ref, cour_ref, smooth_ref, left_ref, right_ref, got_left, got_right, rows_hbm, onto_hbm,
    out_hbm, field_hbm,
    rows_v, out_v, field_v, sem_in, sem_out, sem_field,
):
    owners, ranks, _ = rows_v.shape
    per = owners // PARTS
    spans = [pl.ds(i * per, per) for i in range(PARTS)]
    loads = copies([(rows_hbm.at[s], rows_v.at[s]) for s in spans], sem_in)
    stores = copies([(out_v.at[s], out_hbm.at[s, pl.ds(FIRST, ranks)]) for s in spans], sem_out)
    for c in loads:
        c.start()

    depth, width = smooth_ref.shape
    zeros = jnp.zeros((LANES - 8, depth), jnp.float32)
    lane = iota((depth, LANES), 1)
    at = where_ref[1]
    west = strip(where_ref, got_left[...], left_ref[...], at == 0, False)[8:]
    east = strip(where_ref, right_ref[...], got_right[...], False, at == where_ref[3] - 1)[:8]
    west = jnp.transpose(jnp.concatenate([west, zeros], axis=0))
    east = jnp.transpose(jnp.concatenate([zeros, east], axis=0))
    if width > 2 * LANES:
        field_v[:, LANES : width - LANES] = smooth_ref[:, LANES : width - LANES]
    field_v[:, :LANES] = jnp.where(lane < ITERS, west, smooth_ref[:, :LANES])
    field_v[:, width - LANES :] = jnp.where(lane >= LANES - ITERS, east, smooth_ref[:, width - LANES :])
    store_field = pltpu.make_async_copy(field_v, field_hbm, sem_field)
    store_field.start()

    keep = iota((ranks, LANES), 1) > 0
    for i in range(PARTS):
        loads[i].wait()
        for o in range(i * per, (i + 1) * per):
            x = rows_v[o]
            before = jnp.where(keep, pltpu.roll(x, 1, 1), 0.0)
            out_v[o] = x - cour_ref[FIRST:, o : o + 1] * (x - before)
        stores[i].start()
    store_field.wait()
    for c in stores:
        c.wait()


def finish(where, cour, smoothed, left, right, got_left, got_right, rows, onto):
    hbm = pl.BlockSpec(memory_space=pltpu.HBM)
    vm = pl.BlockSpec(memory_space=pltpu.VMEM)
    return pl.pallas_call(
        finish_kernel,
        in_specs=[pl.BlockSpec(memory_space=pltpu.SMEM)] + [vm] * 6 + [hbm] * 2,
        out_specs=(hbm, hbm),
        out_shape=(
            jax.ShapeDtypeStruct(onto.shape, jnp.float32),
            jax.ShapeDtypeStruct(smoothed.shape, jnp.float32),
        ),
        scratch_shapes=[
            pltpu.VMEM(rows.shape, jnp.float32),
            pltpu.VMEM(rows.shape, jnp.float32),
            pltpu.VMEM(smoothed.shape, jnp.float32),
            pltpu.SemaphoreType.DMA((PARTS,)),
            pltpu.SemaphoreType.DMA((PARTS,)),
            pltpu.SemaphoreType.DMA,
        ],
        input_output_aliases={8: 0},
        compiler_params=params(),
        name="finish",
    )(where, cour, smoothed, left, right, got_left, got_right, rows, onto)


def neighbours(low_part, high_part, axis):
    count = lax.axis_size(axis)
    forward = [(i, i + 1) for i in range(count - 1)]
    backward = [(i + 1, i) for i in range(count - 1)]
    return lax.ppermute(high_part, axis, forward), lax.ppermute(low_part, axis, backward)


def per_device(parcels, growth_rate, cell_index, dest_owner, live_count, supersat, bin_volume):
    owners = lax.axis_size("own")
    total = parcels.shape[0]
    cap = 2 * total // owners
    chunks = total // LANES
    square = lambda x: x.reshape(chunks, LANES)
    exchange = functools.partial(lax.all_to_all, axis_name="own", split_axis=0, concat_axis=0, tiled=True)
    where = jnp.stack([lax.axis_index("grp"), lax.axis_index("own"), lax.axis_size("grp"), owners]).astype(jnp.int32)
    first, src = plan(
        live_count, square(dest_owner), square(growth_rate), square(cell_index), bin_volume.reshape(1, LANES), parcels, owners, cap
    )
    got_first = exchange(first)
    rest = pack(src, parcels)
    got_rest = exchange(rest)

    field, cour, top, bottom, left, right = deposit(got_first, supersat)
    got_up, got_down = neighbours(top, bottom, "grp")
    left, right = sides(got_up, got_down, left, right)
    got_left, got_right = neighbours(left, right, "own")
    smoothed = smooth(where, field, got_up, got_down)
    onto = grow_first(got_first, cour)
    grown, field = finish(where, cour, smoothed, left, right, got_left, got_right, got_rest, onto)
    return grown.reshape(owners * cap, LANES), field


def solution(mesh):
    placed = (
        P(("grp", "own"), None),
        P(("grp", "own")),
        P(("grp", "own")),
        P(("grp", "own")),
        P(("grp", "own")),
        P("grp", "own"),
        P(),
    )
    return jax.shard_map(
        per_device,
        mesh=mesh,
        in_specs=placed,
        out_specs=(P(("grp", "own"), None), P("grp", "own")),
        check_vma=False,
    )
```

```python
import functools

import jax
import jax.numpy as jnp
from jax import lax
from jax.experimental import pallas as pl
from jax.experimental.pallas import tpu as pltpu
from jax.sharding import PartitionSpec as P

ITERS = 4
LANES = 128
FIRST = 16
BATCH = 48
META = 8
NT = (((1,), (1,)), ((), ()))
NN = (((1,), (0,)), ((), ()))
PARTS = 8


def dot(a, b, dims):
    return lax.dot_general(a, b, dims, preferred_element_type=jnp.float32)


def split3(x):
    hi = x.astype(jnp.bfloat16).astype(jnp.float32)
    rest = x - hi
    mid = rest.astype(jnp.bfloat16).astype(jnp.float32)
    return hi, mid, rest - mid


def iota(shape, dim):
    return lax.broadcasted_iota(jnp.int32, shape, dim)


def params(mib):
    return pltpu.CompilerParams(vmem_limit_bytes=mib << 20)


def copies(pairs, sems):
    return [pltpu.make_async_copy(a, b, sems.at[i]) for i, (a, b) in enumerate(pairs)]


def plan_kernel(
    live_ref, dest_hbm, rate_hbm, cell_hbm, vol_hbm, rows_hbm,
    first_hbm, src_ref,
    dest_ref, rate_ref, cell_ref, vol_ref, rows_v, first_ref, lhs, bt, vrow, src_smem, sem_in, sem_src, sem_out,
):
    chunks = dest_ref.shape[0]
    owners, cap = src_ref.shape
    total = chunks * LANES
    loads = copies(
        [
            (dest_hbm, dest_ref),
            (rows_hbm, rows_v.at[pl.ds(0, total)]),
            (vol_hbm, vol_ref),
            (rate_hbm, rate_ref),
            (cell_hbm, cell_ref),
        ],
        sem_in,
    )
    for c in loads:
        c.start()
    rows_v[total : total + 8, :] = jnp.zeros((8, LANES), jnp.float32)
    loads[0].wait()

    live = live_ref[0]
    lane = iota((1, LANES), 1)
    owner_of = iota((owners, LANES), 0)
    tri = (iota((LANES, 2 * LANES), 0) <= iota((LANES, 2 * LANES), 1)).astype(jnp.bfloat16)
    hits = []
    for s in range(chunks):
        target = jnp.where(lane + s * LANES < live, dest_ref[s : s + 1, :], -1)
        hits.append((owner_of == target).astype(jnp.float32))
    counts = dot(jnp.concatenate(hits, axis=0).astype(jnp.bfloat16), tri, NN)

    for c in loads[1:]:
        c.wait()
    vol = vol_ref[...]
    shifted = jnp.where(lane == LANES - 1, 0.0, pltpu.roll(vol, LANES - 1, 1))
    w_hi, w_mid, w_lo = split3(vol - shifted)
    weights = jnp.concatenate(
        [w_hi, w_mid, w_lo, jnp.zeros((5, LANES), jnp.float32)], axis=0
    ).astype(jnp.bfloat16)
    span = 512
    for s in range(total // span):
        r_hi, r_mid, r_lo = split3(rows_v[s * span : (s + 1) * span, :])
        p_hi = dot(weights, r_hi.astype(jnp.bfloat16), NT)
        p_mid = dot(weights, r_mid.astype(jnp.bfloat16), NT)
        p_lo = dot(weights, r_lo.astype(jnp.bfloat16), NT)
        v = p_hi[0:1] + (p_hi[1:2] + p_mid[0:1]) + (p_hi[2:3] + p_mid[1:2] + p_lo[0:1])
        vrow[:, s * span : (s + 1) * span] = v

    rank_of = iota((cap, LANES), 0).astype(jnp.float32)
    ranks = []
    carry = jnp.zeros((owners, LANES), jnp.float32)
    for s in range(chunks):
        hit = hits[s]
        part = counts[s * owners : (s + 1) * owners]
        rank = jnp.sum(hit * (part[:, :LANES] + carry - 1.0), axis=0, keepdims=True)
        carry = carry + part[:, LANES:]
        cols = slice(s * LANES, (s + 1) * LANES)
        ranks.append(rank)
        cell = cell_ref[s : s + 1, :]
        cell_hi = jnp.right_shift(cell + 256, 9)
        cell_lo = cell - cell_hi * 512
        values = (
            (jnp.full((1, LANES), s + 1, jnp.float32), lane.astype(jnp.float32))
            + split3(rate_ref[s : s + 1, :])
            + (cell_hi.astype(jnp.float32), cell_lo.astype(jnp.float32))
            + split3(vrow[:, cols])
        )
        for q, value in enumerate(values):
            lhs[q * owners : (q + 1) * owners, cols] = (hit * value).astype(jnp.bfloat16)

    turned = jnp.transpose(jnp.concatenate(ranks + [jnp.zeros((LANES - chunks, LANES), jnp.float32)], axis=0))
    across = iota((LANES, cap), 1).astype(jnp.float32)
    for s in range(chunks):
        bt[s * LANES : (s + 1) * LANES, :] = (across == turned[:, s : s + 1]).astype(jnp.float32).astype(jnp.bfloat16)
    packed = dot(lhs[...], bt[...], NN)
    part = [packed[q * owners : (q + 1) * owners] for q in range(10)]
    src = jnp.where(part[0] > 0.5, (part[0] - 1.0) * LANES + part[1], float(total))
    src_ref[...] = src.astype(jnp.int32)
    to_smem = pltpu.make_async_copy(src_ref, src_smem, sem_src)
    to_smem.start()
    meta = (
        part[2] + part[3] + part[4],
        part[5] * 512.0 + part[6],
        part[7] + part[8] + part[9],
    )
    first = first_ref.shape[1] - META
    for q, value in enumerate(meta):
        for half in range(2):
            at = first + 2 * q + half
            for j in range(owners):
                first_ref[j, at : at + 1, :] = value[j : j + 1, half * LANES : (half + 1) * LANES]
    for j in range(owners):
        first_ref[j, first + 6 : first + 8, :] = jnp.zeros((2, LANES), jnp.float32)
    to_smem.wait()

    def copy_rows(j, _):
        at = [src_smem[j, r] for r in range(first)]
        rows = [rows_v[pl.ds(i, 1), :] for i in at]
        for r in range(first):
            first_ref[j, r : r + 1, :] = rows[r]
        return 0

    per = owners // PARTS
    spans = [pl.ds(i * per, per) for i in range(PARTS)]
    stores = copies([(first_ref.at[s], first_hbm.at[s]) for s in spans], sem_out)
    for i in range(PARTS):
        lax.fori_loop(i * per, (i + 1) * per, copy_rows, 0)
        stores[i].start()
    for c in stores:
        c.wait()


def plan(live, dest, rate, cell, vol, rows, owners, cap):
    chunks = dest.shape[0]
    total = chunks * LANES
    hbm = pl.BlockSpec(memory_space=pltpu.HBM)
    return pl.pallas_call(
        plan_kernel,
        in_specs=[pl.BlockSpec(memory_space=pltpu.SMEM)] + [hbm] * 5,
        out_specs=(hbm, pl.BlockSpec(memory_space=pltpu.VMEM)),
        out_shape=(
            jax.ShapeDtypeStruct((owners, FIRST + META, LANES), jnp.float32),
            jax.ShapeDtypeStruct((owners, cap), jnp.int32),
        ),
        scratch_shapes=[
            pltpu.VMEM((chunks, LANES), jnp.int32),
            pltpu.VMEM((chunks, LANES), jnp.float32),
            pltpu.VMEM((chunks, LANES), jnp.int32),
            pltpu.VMEM((1, LANES), jnp.float32),
            pltpu.VMEM((total + 8, LANES), jnp.float32),
            pltpu.VMEM((owners, FIRST + META, LANES), jnp.float32),
            pltpu.VMEM((10 * owners, total), jnp.bfloat16),
            pltpu.VMEM((total, cap), jnp.bfloat16),
            pltpu.VMEM((1, total), jnp.float32),
            pltpu.SMEM((owners, cap), jnp.int32),
            pltpu.SemaphoreType.DMA((5,)),
            pltpu.SemaphoreType.DMA,
            pltpu.SemaphoreType.DMA((PARTS,)),
        ],
        compiler_params=params(60),
        name="plan",
    )(live, dest, rate, cell, vol, rows)


def pack_kernel(src_ref, rows_hbm, out_hbm, rows_v, out_v, sem_rows, sem_out):
    total = rows_v.shape[0] - 8
    owners, ranks, _ = out_v.shape
    load = pltpu.make_async_copy(rows_hbm, rows_v.at[pl.ds(0, total)], sem_rows)
    load.start()
    rows_v[total : total + 8, :] = jnp.zeros((8, LANES), jnp.float32)

    def clear(j, _):
        out_v[j] = jnp.zeros((ranks, LANES), jnp.float32)
        return 0

    lax.fori_loop(0, owners, clear, 0)
    load.wait()
    per = owners // PARTS
    spans = [pl.ds(i * per, per) for i in range(PARTS)]
    stores = copies([(out_v.at[s], out_hbm.at[s]) for s in spans], sem_out)

    def copy_rows(j, _):
        for base in range(0, ranks, BATCH):
            @pl.when(src_ref[j, FIRST + base] < total)
            def _():
                at = [src_ref[j, FIRST + base + r] for r in range(BATCH)]
                rows = [rows_v[pl.ds(i, 1), :] for i in at]
                for r in range(BATCH):
                    out_v[j, base + r : base + r + 1, :] = rows[r]

        return 0

    for i in range(PARTS):
        lax.fori_loop(i * per, (i + 1) * per, copy_rows, 0)
        stores[i].start()
    for c in stores:
        c.wait()


def pack(src, rows):
    owners, cap = src.shape
    total = rows.shape[0]
    hbm = pl.BlockSpec(memory_space=pltpu.HBM)
    shape = (owners, cap - FIRST, LANES)
    return pl.pallas_call(
        pack_kernel,
        in_specs=[pl.BlockSpec(memory_space=pltpu.SMEM), hbm],
        out_specs=hbm,
        out_shape=jax.ShapeDtypeStruct(shape, jnp.float32),
        scratch_shapes=[
            pltpu.VMEM((total + 8, LANES), jnp.float32),
            pltpu.VMEM(shape, jnp.float32),
            pltpu.SemaphoreType.DMA,
            pltpu.SemaphoreType.DMA((PARTS,)),
        ],
        compiler_params=params(60),
        cost_estimate=pl.CostEstimate(flops=0, bytes_accessed=24 << 20, transcendentals=0),
        name="pack",
    )(src, rows)


def deposit_kernel(
    first_hbm, sup_hbm, field_ref, cour_ref, top_ref, bottom_ref, left_ref, right_ref,
    meta_ref, sup_ref, table, high, acc, cour, sem,
):
    depth, width = sup_ref.shape
    owners = meta_ref.shape[0]
    loads = copies([(sup_hbm, sup_ref), (first_hbm.at[:, pl.ds(FIRST, META)], meta_ref)], sem)
    for c in loads:
        c.start()
    for c in loads:
        c.wait()
    group = 4
    n = group * 2 * LANES
    flipped = jnp.transpose(sup_ref[...])
    f_hi = flipped.astype(jnp.bfloat16)
    table[:width, :] = f_hi
    table[width:, :] = (flipped - f_hi.astype(jnp.float32)).astype(jnp.bfloat16)
    acc[...] = jnp.zeros_like(acc)

    def step(g, _):
        def lane_row(q):
            return jnp.concatenate(
                [meta_ref[g * group + o, 2 * q + half : 2 * q + half + 1, :] for o in range(group) for half in range(2)],
                axis=1,
            )

        rate, cell, v = lane_row(0), lane_row(1).astype(jnp.int32), lane_row(2)
        row_at = jnp.right_shift(cell, 8)
        col_at = jnp.bitwise_and(cell, 255)
        high[...] = (iota((depth, n), 0) == row_at).astype(jnp.float32).astype(jnp.bfloat16)
        lines = dot(table[...], high[...], NN)
        across = iota((width, n), 0) == col_at
        sat = jnp.sum(jnp.where(across, lines[:width] + lines[width:], 0.0), axis=0, keepdims=True)
        courant = rate * sat
        for o in range(group):
            cour[pl.ds(g * group + o, 1), :] = courant[:, o * 2 * LANES : (o + 1) * 2 * LANES]
        mass = courant * v
        m_hi = mass.astype(jnp.bfloat16).astype(jnp.float32)
        spread = jnp.concatenate(
            [jnp.where(across, m_hi, 0.0).astype(jnp.bfloat16), jnp.where(across, mass - m_hi, 0.0).astype(jnp.bfloat16)],
            axis=0,
        )
        acc[...] += dot(high[...], spread, NT)
        return 0

    lax.fori_loop(0, owners // group, step, 0)
    field = sup_ref[...] - 0.5 * (acc[:, :width] + acc[:, width:])
    field_ref[...] = field
    cour_ref[...] = jnp.transpose(cour[...])
    top_ref[...] = field[:8]
    bottom_ref[...] = field[depth - 8 :]
    left_ref[...] = jnp.transpose(field[:, :LANES])[:8]
    right_ref[...] = jnp.transpose(field[:, width - LANES :])[LANES - 8 :]


def deposit(got_first, supersat):
    owners = got_first.shape[0]
    depth, width = supersat.shape
    f32 = jnp.float32
    vm = pl.BlockSpec(memory_space=pltpu.VMEM)
    hbm = pl.BlockSpec(memory_space=pltpu.HBM)
    outs = [(depth, width), (2 * LANES, owners), (8, width), (8, width), (8, depth), (8, depth)]
    return pl.pallas_call(
        deposit_kernel,
        in_specs=[hbm, hbm],
        out_specs=[vm] * len(outs),
        out_shape=[jax.ShapeDtypeStruct(s, f32) for s in outs],
        scratch_shapes=[
            pltpu.VMEM((owners, META, LANES), f32),
            pltpu.VMEM((depth, width), f32),
            pltpu.VMEM((2 * width, depth), jnp.bfloat16),
            pltpu.VMEM((depth, 8 * LANES), jnp.bfloat16),
            pltpu.VMEM((depth, 2 * width), f32),
            pltpu.VMEM((owners, 2 * LANES), f32),
            pltpu.SemaphoreType.DMA((2,)),
        ],
        compiler_params=params(16),
        cost_estimate=pl.CostEstimate(flops=9 << 30, bytes_accessed=8 << 20, transcendentals=0),
        name="deposit",
    )(got_first, supersat)


def sides_kernel(up_ref, down_ref, left_ref, right_ref, out_left, out_right):
    depth = left_ref.shape[1]
    width = up_ref.shape[1]
    lane = iota((8, LANES), 1)
    for out, own_ref, begin in ((out_left, left_ref, 0), (out_right, right_ref, width - LANES)):
        skip = 0 if begin == 0 else LANES - 8
        ends = jnp.concatenate([up_ref[:, begin : begin + LANES], down_ref[:, begin : begin + LANES]], axis=0)
        ends = jnp.concatenate([ends, jnp.zeros((LANES - 16, LANES), jnp.float32)], axis=0)
        ends = jnp.transpose(ends)[skip : skip + 8]
        out[:, : depth] = own_ref[...]
        out[:, depth:] = jnp.where(lane < 16, ends, 0.0)


def sides(up, down, left, right):
    shape = (8, left.shape[1] + LANES)
    return pl.pallas_call(
        sides_kernel,
        out_shape=[jax.ShapeDtypeStruct(shape, jnp.float32)] * 2,
        compiler_params=params(4),
        name="sides",
    )(up, down, left, right)


def passes(x, inside):
    tall, wide = x.shape
    for _ in range(ITERS):
        beside = pltpu.roll(x, tall - 1, 0) + pltpu.roll(x, 1, 0) + pltpu.roll(x, wide - 1, 1) + pltpu.roll(x, 1, 1)
        x = jnp.where(inside, x + 0.2 * (beside - 4.0 * x), 0.0)
    return x


def smooth_kernel(where_ref, field_ref, up_ref, down_ref, out_ref):
    depth, width = field_ref.shape
    x = jnp.concatenate([up_ref[...], field_ref[...], down_ref[...]], axis=0)
    row = iota(x.shape, 0)
    inside = (row >= jnp.where(where_ref[0] == 0, 8, 0)) & (
        row < jnp.where(where_ref[0] == where_ref[2] - 1, 8 + depth, 16 + depth)
    )
    out_ref[...] = passes(x, inside)[8 : 8 + depth]


def smooth(where, field, up, down):
    vm = pl.BlockSpec(memory_space=pltpu.VMEM)
    return pl.pallas_call(
        smooth_kernel,
        in_specs=[pl.BlockSpec(memory_space=pltpu.SMEM)] + [vm] * 3,
        out_specs=vm,
        out_shape=jax.ShapeDtypeStruct(field.shape, jnp.float32),
        compiler_params=params(8),
        name="smooth",
    )(where, field, up, down)


def strip(where_ref, low, high, low_out, high_out):
    depth = low.shape[1] - LANES
    x = jnp.concatenate([low, high], axis=0)
    tail = x[:, depth:]
    lane = iota(tail.shape, 1)
    above = jnp.where(lane >= LANES - 8, pltpu.roll(tail, LANES - 8, 1), 0.0)
    below = jnp.where(lane < 8, pltpu.roll(tail, LANES - 8, 1), 0.0)
    x = jnp.concatenate([above, x[:, :depth], below], axis=1)
    row, col = iota(x.shape, 0), iota(x.shape, 1)
    inside = (
        (row >= jnp.where(low_out, 8, 0))
        & (row < jnp.where(high_out, 8, 16))
        & (col >= jnp.where(where_ref[0] == 0, LANES, 0))
        & (col < jnp.where(where_ref[0] == where_ref[2] - 1, LANES + depth, 2 * LANES + depth))
    )
    return passes(x, inside)[:, LANES : LANES + depth]


def grown_by(x, courant):
    keep = iota(x.shape, 1) > 0
    return x - courant * (x - jnp.where(keep, pltpu.roll(x, 1, 1), 0.0))


def grow_first_kernel(cour_ref, first_hbm, out_hbm, rows_v, out_v, sem):
    owners, ranks, _ = rows_v.shape
    load, store = copies([(first_hbm.at[:, pl.ds(0, ranks)], rows_v), (out_v, out_hbm.at[:, pl.ds(0, ranks)])], sem)
    load.start()
    load.wait()
    for o in range(owners):
        out_v[o] = grown_by(rows_v[o], cour_ref[:ranks, o : o + 1])
    store.start()
    store.wait()


def grow_first(rows, cour):
    cap, owners = cour.shape
    hbm = pl.BlockSpec(memory_space=pltpu.HBM)
    return pl.pallas_call(
        grow_first_kernel,
        in_specs=[pl.BlockSpec(memory_space=pltpu.VMEM), hbm],
        out_specs=hbm,
        out_shape=jax.ShapeDtypeStruct((owners, cap, LANES), jnp.float32),
        scratch_shapes=[
            pltpu.VMEM((owners, FIRST, LANES), jnp.float32),
            pltpu.VMEM((owners, FIRST, LANES), jnp.float32),
            pltpu.SemaphoreType.DMA((2,)),
        ],
        compiler_params=params(8),
        name="grow_first",
    )(cour, rows)


def finish_kernel(
    where_ref, cour_ref, smooth_ref, left_ref, right_ref, got_left, got_right, rows_hbm, onto_hbm,
    out_hbm, field_hbm,
    rows_v, out_v, field_v, sem_in, sem_out, sem_field,
):
    owners, ranks, _ = rows_v.shape
    per = owners // PARTS
    spans = [pl.ds(i * per, per) for i in range(PARTS)]
    loads = copies([(rows_hbm.at[s], rows_v.at[s]) for s in spans], sem_in)
    stores = copies([(out_v.at[s], out_hbm.at[s, pl.ds(FIRST, ranks)]) for s in spans], sem_out)
    for c in loads:
        c.start()

    depth, width = smooth_ref.shape
    zeros = jnp.zeros((LANES - 8, depth), jnp.float32)
    lane = iota((depth, LANES), 1)
    at = where_ref[1]
    west = strip(where_ref, got_left[...], left_ref[...], at == 0, False)[8:]
    east = strip(where_ref, right_ref[...], got_right[...], False, at == where_ref[3] - 1)[:8]
    west = jnp.transpose(jnp.concatenate([west, zeros], axis=0))
    east = jnp.transpose(jnp.concatenate([zeros, east], axis=0))
    if width > 2 * LANES:
        field_v[:, LANES : width - LANES] = smooth_ref[:, LANES : width - LANES]
    field_v[:, :LANES] = jnp.where(lane < ITERS, west, smooth_ref[:, :LANES])
    field_v[:, width - LANES :] = jnp.where(lane >= LANES - ITERS, east, smooth_ref[:, width - LANES :])
    store_field = pltpu.make_async_copy(field_v, field_hbm, sem_field)
    store_field.start()

    for i in range(PARTS):
        loads[i].wait()
        for o in range(i * per, (i + 1) * per):
            out_v[o] = grown_by(rows_v[o], cour_ref[FIRST:, o : o + 1])
        stores[i].start()
    store_field.wait()
    for c in stores:
        c.wait()


def finish(where, cour, smoothed, left, right, got_left, got_right, rows, onto):
    hbm = pl.BlockSpec(memory_space=pltpu.HBM)
    vm = pl.BlockSpec(memory_space=pltpu.VMEM)
    return pl.pallas_call(
        finish_kernel,
        in_specs=[pl.BlockSpec(memory_space=pltpu.SMEM)] + [vm] * 6 + [hbm] * 2,
        out_specs=(hbm, hbm),
        out_shape=(
            jax.ShapeDtypeStruct(onto.shape, jnp.float32),
            jax.ShapeDtypeStruct(smoothed.shape, jnp.float32),
        ),
        scratch_shapes=[
            pltpu.VMEM(rows.shape, jnp.float32),
            pltpu.VMEM(rows.shape, jnp.float32),
            pltpu.VMEM(smoothed.shape, jnp.float32),
            pltpu.SemaphoreType.DMA((PARTS,)),
            pltpu.SemaphoreType.DMA((PARTS,)),
            pltpu.SemaphoreType.DMA,
        ],
        input_output_aliases={8: 0},
        compiler_params=params(16),
        name="finish",
    )(where, cour, smoothed, left, right, got_left, got_right, rows, onto)


def neighbours(low_part, high_part, axis):
    count = lax.axis_size(axis)
    forward = [(i, i + 1) for i in range(count - 1)]
    backward = [(i + 1, i) for i in range(count - 1)]
    return lax.ppermute(high_part, axis, forward), lax.ppermute(low_part, axis, backward)


def per_device(parcels, growth_rate, cell_index, dest_owner, live_count, supersat, bin_volume):
    owners = lax.axis_size("own")
    total = parcels.shape[0]
    cap = 2 * total // owners
    chunks = total // LANES
    square = lambda x: x.reshape(chunks, LANES)
    exchange = functools.partial(lax.all_to_all, axis_name="own", split_axis=0, concat_axis=0, tiled=True)
    where = jnp.stack([lax.axis_index("grp"), lax.axis_index("own"), lax.axis_size("grp"), owners]).astype(jnp.int32)
    first, src = plan(
        live_count, square(dest_owner), square(growth_rate), square(cell_index), bin_volume.reshape(1, LANES), parcels, owners, cap
    )
    got_first = exchange(first)
    rest = pack(src, parcels)
    got_rest = exchange(rest)

    field, cour, top, bottom, left, right = deposit(got_first, supersat)
    got_up, got_down = neighbours(top, bottom, "grp")
    left, right = sides(got_up, got_down, left, right)
    got_left, got_right = neighbours(left, right, "own")
    smoothed = smooth(where, field, got_up, got_down)
    onto = grow_first(got_first, cour)
    grown, field = finish(where, cour, smoothed, left, right, got_left, got_right, got_rest, onto)
    return grown.reshape(owners * cap, LANES), field


def solution(mesh):
    placed = (
        P(("grp", "own"), None),
        P(("grp", "own")),
        P(("grp", "own")),
        P(("grp", "own")),
        P(("grp", "own")),
        P("grp", "own"),
        P(),
    )
    return jax.shard_map(
        per_device,
        mesh=mesh,
        in_specs=placed,
        out_specs=(P(("grp", "own"), None), P("grp", "own")),
        check_vma=False,
    )
```

```python
import functools

import jax
import jax.numpy as jnp
from jax import lax
from jax.experimental import pallas as pl
from jax.experimental.pallas import tpu as pltpu
from jax.sharding import PartitionSpec as P

ITERS = 4
LANES = 128
FIRST = 24
BATCH = 116
META = 8
NT = (((1,), (1,)), ((), ()))
NN = (((1,), (0,)), ((), ()))
PARTS = 8


def dot(a, b, dims):
    return lax.dot_general(a, b, dims, preferred_element_type=jnp.float32)


def split3(x):
    hi = x.astype(jnp.bfloat16).astype(jnp.float32)
    rest = x - hi
    mid = rest.astype(jnp.bfloat16).astype(jnp.float32)
    return hi, mid, rest - mid


def iota(shape, dim):
    return lax.broadcasted_iota(jnp.int32, shape, dim)


def params(mib):
    return pltpu.CompilerParams(vmem_limit_bytes=mib << 20)


def copies(pairs, sems):
    return [pltpu.make_async_copy(a, b, sems.at[i]) for i, (a, b) in enumerate(pairs)]


def plan_kernel(
    live_ref, dest_hbm, rate_hbm, cell_hbm, vol_hbm, rows_hbm,
    first_hbm, src_ref,
    dest_ref, rate_ref, cell_ref, vol_ref, rows_v, first_ref, lhs, bt, vrow, src_smem, sem_in, sem_src, sem_out,
):
    chunks = dest_ref.shape[0]
    owners, cap = src_ref.shape
    total = chunks * LANES
    loads = copies(
        [
            (dest_hbm, dest_ref),
            (rows_hbm, rows_v.at[pl.ds(0, total)]),
            (vol_hbm, vol_ref),
            (rate_hbm, rate_ref),
            (cell_hbm, cell_ref),
        ],
        sem_in,
    )
    for c in loads:
        c.start()
    rows_v[total : total + 8, :] = jnp.zeros((8, LANES), jnp.float32)
    loads[0].wait()

    live = live_ref[0]
    lane = iota((1, LANES), 1)
    owner_of = iota((owners, LANES), 0)
    tri = (iota((LANES, 2 * LANES), 0) <= iota((LANES, 2 * LANES), 1)).astype(jnp.bfloat16)
    hits = []
    for s in range(chunks):
        target = jnp.where(lane + s * LANES < live, dest_ref[s : s + 1, :], -1)
        hits.append((owner_of == target).astype(jnp.float32))
    counts = dot(jnp.concatenate(hits, axis=0).astype(jnp.bfloat16), tri, NN)

    for c in loads[1:]:
        c.wait()
    vol = vol_ref[...]
    shifted = jnp.where(lane == LANES - 1, 0.0, pltpu.roll(vol, LANES - 1, 1))
    w_hi, w_mid, w_lo = split3(vol - shifted)
    weights = jnp.concatenate(
        [w_hi, w_mid, w_lo, jnp.zeros((5, LANES), jnp.float32)], axis=0
    ).astype(jnp.bfloat16)
    span = 512
    for s in range(total // span):
        r_hi, r_mid, r_lo = split3(rows_v[s * span : (s + 1) * span, :])
        p_hi = dot(weights, r_hi.astype(jnp.bfloat16), NT)
        p_mid = dot(weights, r_mid.astype(jnp.bfloat16), NT)
        p_lo = dot(weights, r_lo.astype(jnp.bfloat16), NT)
        v = p_hi[0:1] + (p_hi[1:2] + p_mid[0:1]) + (p_hi[2:3] + p_mid[1:2] + p_lo[0:1])
        vrow[:, s * span : (s + 1) * span] = v

    rank_of = iota((cap, LANES), 0).astype(jnp.float32)
    ranks = []
    carry = jnp.zeros((owners, LANES), jnp.float32)
    for s in range(chunks):
        hit = hits[s]
        part = counts[s * owners : (s + 1) * owners]
        rank = jnp.sum(hit * (part[:, :LANES] + carry - 1.0), axis=0, keepdims=True)
        carry = carry + part[:, LANES:]
        cols = slice(s * LANES, (s + 1) * LANES)
        ranks.append(rank)
        cell = cell_ref[s : s + 1, :]
        cell_hi = jnp.right_shift(cell + 256, 9)
        cell_lo = cell - cell_hi * 512
        values = (
            (jnp.full((1, LANES), s + 1, jnp.float32), lane.astype(jnp.float32))
            + split3(rate_ref[s : s + 1, :])
            + (cell_hi.astype(jnp.float32), cell_lo.astype(jnp.float32))
            + split3(vrow[:, cols])
        )
        for q, value in enumerate(values):
            lhs[q * owners : (q + 1) * owners, cols] = (hit * value).astype(jnp.bfloat16)

    turned = jnp.transpose(jnp.concatenate(ranks + [jnp.zeros((LANES - chunks, LANES), jnp.float32)], axis=0))
    across = iota((LANES, cap), 1).astype(jnp.float32)
    for s in range(chunks):
        bt[s * LANES : (s + 1) * LANES, :] = (across == turned[:, s : s + 1]).astype(jnp.float32).astype(jnp.bfloat16)
    packed = dot(lhs[...], bt[...], NN)
    part = [packed[q * owners : (q + 1) * owners] for q in range(10)]
    src = jnp.where(part[0] > 0.5, (part[0] - 1.0) * LANES + part[1], float(total))
    src_ref[...] = src.astype(jnp.int32)
    to_smem = pltpu.make_async_copy(src_ref, src_smem, sem_src)
    to_smem.start()
    meta = (
        part[2] + part[3] + part[4],
        part[5] * 512.0 + part[6],
        part[7] + part[8] + part[9],
    )
    first = first_ref.shape[1] - META
    for q, value in enumerate(meta):
        for half in range(2):
            at = first + 2 * q + half
            for j in range(owners):
                first_ref[j, at : at + 1, :] = value[j : j + 1, half * LANES : (half + 1) * LANES]
    for j in range(owners):
        first_ref[j, first + 6 : first + 8, :] = jnp.zeros((2, LANES), jnp.float32)
    to_smem.wait()

    def copy_rows(j, _):
        at = [src_smem[j, r] for r in range(first)]
        rows = [rows_v[pl.ds(i, 1), :] for i in at]
        for r in range(first):
            first_ref[j, r : r + 1, :] = rows[r]
        return 0

    per = owners // PARTS
    spans = [pl.ds(i * per, per) for i in range(PARTS)]
    stores = copies([(first_ref.at[s], first_hbm.at[s]) for s in spans], sem_out)
    for i in range(PARTS):
        lax.fori_loop(i * per, (i + 1) * per, copy_rows, 0)
        stores[i].start()
    for c in stores:
        c.wait()


def plan(live, dest, rate, cell, vol, rows, owners, cap):
    chunks = dest.shape[0]
    total = chunks * LANES
    hbm = pl.BlockSpec(memory_space=pltpu.HBM)
    return pl.pallas_call(
        plan_kernel,
        in_specs=[pl.BlockSpec(memory_space=pltpu.SMEM)] + [hbm] * 5,
        out_specs=(hbm, pl.BlockSpec(memory_space=pltpu.VMEM)),
        out_shape=(
            jax.ShapeDtypeStruct((owners, FIRST + META, LANES), jnp.float32),
            jax.ShapeDtypeStruct((owners, cap), jnp.int32),
        ),
        scratch_shapes=[
            pltpu.VMEM((chunks, LANES), jnp.int32),
            pltpu.VMEM((chunks, LANES), jnp.float32),
            pltpu.VMEM((chunks, LANES), jnp.int32),
            pltpu.VMEM((1, LANES), jnp.float32),
            pltpu.VMEM((total + 8, LANES), jnp.float32),
            pltpu.VMEM((owners, FIRST + META, LANES), jnp.float32),
            pltpu.VMEM((10 * owners, total), jnp.bfloat16),
            pltpu.VMEM((total, cap), jnp.bfloat16),
            pltpu.VMEM((1, total), jnp.float32),
            pltpu.SMEM((owners, cap), jnp.int32),
            pltpu.SemaphoreType.DMA((5,)),
            pltpu.SemaphoreType.DMA,
            pltpu.SemaphoreType.DMA((PARTS,)),
        ],
        compiler_params=params(60),
        name="plan",
    )(live, dest, rate, cell, vol, rows)


def pack_kernel(src_ref, rows_hbm, out_hbm, rows_v, out_v, sem_rows, sem_out):
    total = rows_v.shape[0] - 8
    owners, ranks, _ = out_v.shape
    load = pltpu.make_async_copy(rows_hbm, rows_v.at[pl.ds(0, total)], sem_rows)
    load.start()
    rows_v[total : total + 8, :] = jnp.zeros((8, LANES), jnp.float32)

    def clear(j, _):
        out_v[j] = jnp.zeros((ranks, LANES), jnp.float32)
        return 0

    lax.fori_loop(0, owners, clear, 0)
    load.wait()
    per = owners // PARTS
    spans = [pl.ds(i * per, per) for i in range(PARTS)]
    stores = copies([(out_v.at[s], out_hbm.at[s]) for s in spans], sem_out)

    def copy_rows(j, _):
        for base in range(0, ranks, BATCH):
            @pl.when(src_ref[j, FIRST + base] < total)
            def _():
                at = [src_ref[j, FIRST + base + r] for r in range(BATCH)]
                rows = [rows_v[pl.ds(i, 1), :] for i in at]
                for r in range(BATCH):
                    out_v[j, base + r : base + r + 1, :] = rows[r]

        return 0

    for i in range(PARTS):
        lax.fori_loop(i * per, (i + 1) * per, copy_rows, 0)
        stores[i].start()
    for c in stores:
        c.wait()


def pack(src, rows):
    owners, cap = src.shape
    total = rows.shape[0]
    hbm = pl.BlockSpec(memory_space=pltpu.HBM)
    shape = (owners, cap - FIRST, LANES)
    return pl.pallas_call(
        pack_kernel,
        in_specs=[pl.BlockSpec(memory_space=pltpu.SMEM), hbm],
        out_specs=hbm,
        out_shape=jax.ShapeDtypeStruct(shape, jnp.float32),
        scratch_shapes=[
            pltpu.VMEM((total + 8, LANES), jnp.float32),
            pltpu.VMEM(shape, jnp.float32),
            pltpu.SemaphoreType.DMA,
            pltpu.SemaphoreType.DMA((PARTS,)),
        ],
        compiler_params=params(60),
        cost_estimate=pl.CostEstimate(flops=0, bytes_accessed=24 << 20, transcendentals=0),
        name="pack",
    )(src, rows)


def deposit_kernel(
    first_hbm, sup_hbm, field_ref, cour_ref, top_ref, bottom_ref, left_ref, right_ref,
    meta_ref, sup_ref, table, high, acc, cour, sem,
):
    depth, width = sup_ref.shape
    owners = meta_ref.shape[0]
    loads = copies([(sup_hbm, sup_ref), (first_hbm.at[:, pl.ds(FIRST, META)], meta_ref)], sem)
    for c in loads:
        c.start()
    for c in loads:
        c.wait()
    group = 4
    n = group * 2 * LANES
    flipped = jnp.transpose(sup_ref[...])
    f_hi = flipped.astype(jnp.bfloat16)
    table[:width, :] = f_hi
    table[width:, :] = (flipped - f_hi.astype(jnp.float32)).astype(jnp.bfloat16)
    acc[...] = jnp.zeros_like(acc)

    def step(g, _):
        def lane_row(q):
            return jnp.concatenate(
                [meta_ref[g * group + o, 2 * q + half : 2 * q + half + 1, :] for o in range(group) for half in range(2)],
                axis=1,
            )

        rate, cell, v = lane_row(0), lane_row(1).astype(jnp.int32), lane_row(2)
        row_at = jnp.right_shift(cell, 8)
        col_at = jnp.bitwise_and(cell, 255)
        high[...] = (iota((depth, n), 0) == row_at).astype(jnp.float32).astype(jnp.bfloat16)
        lines = dot(table[...], high[...], NN)
        across = iota((width, n), 0) == col_at
        sat = jnp.sum(jnp.where(across, lines[:width] + lines[width:], 0.0), axis=0, keepdims=True)
        courant = rate * sat
        for o in range(group):
            cour[pl.ds(g * group + o, 1), :] = courant[:, o * 2 * LANES : (o + 1) * 2 * LANES]
        mass = courant * v
        m_hi = mass.astype(jnp.bfloat16).astype(jnp.float32)
        spread = jnp.concatenate(
            [jnp.where(across, m_hi, 0.0).astype(jnp.bfloat16), jnp.where(across, mass - m_hi, 0.0).astype(jnp.bfloat16)],
            axis=0,
        )
        acc[...] += dot(high[...], spread, NT)
        return 0

    lax.fori_loop(0, owners // group, step, 0)
    field = sup_ref[...] - 0.5 * (acc[:, :width] + acc[:, width:])
    field_ref[...] = field
    cour_ref[...] = jnp.transpose(jnp.concatenate(split3(cour[...]) + (jnp.zeros_like(cour),), axis=0))
    top_ref[...] = field[:8]
    bottom_ref[...] = field[depth - 8 :]
    left_ref[...] = jnp.transpose(field[:, :LANES])[:8]
    right_ref[...] = jnp.transpose(field[:, width - LANES :])[LANES - 8 :]


def deposit(got_first, supersat):
    owners = got_first.shape[0]
    depth, width = supersat.shape
    f32 = jnp.float32
    vm = pl.BlockSpec(memory_space=pltpu.VMEM)
    hbm = pl.BlockSpec(memory_space=pltpu.HBM)
    outs = [(depth, width), (2 * LANES, 4 * owners), (8, width), (8, width), (8, depth), (8, depth)]
    return pl.pallas_call(
        deposit_kernel,
        in_specs=[hbm, hbm],
        out_specs=[vm] * len(outs),
        out_shape=[jax.ShapeDtypeStruct(s, f32) for s in outs],
        scratch_shapes=[
            pltpu.VMEM((owners, META, LANES), f32),
            pltpu.VMEM((depth, width), f32),
            pltpu.VMEM((2 * width, depth), jnp.bfloat16),
            pltpu.VMEM((depth, 8 * LANES), jnp.bfloat16),
            pltpu.VMEM((depth, 2 * width), f32),
            pltpu.VMEM((owners, 2 * LANES), f32),
            pltpu.SemaphoreType.DMA((2,)),
        ],
        compiler_params=params(16),
        cost_estimate=pl.CostEstimate(flops=9 << 30, bytes_accessed=8 << 20, transcendentals=0),
        name="deposit",
    )(got_first, supersat)


def sides_kernel(up_ref, down_ref, left_ref, right_ref, out_left, out_right):
    depth = left_ref.shape[1]
    width = up_ref.shape[1]
    lane = iota((8, LANES), 1)
    for out, own_ref, begin in ((out_left, left_ref, 0), (out_right, right_ref, width - LANES)):
        skip = 0 if begin == 0 else LANES - 8
        ends = jnp.concatenate([up_ref[:, begin : begin + LANES], down_ref[:, begin : begin + LANES]], axis=0)
        ends = jnp.concatenate([ends, jnp.zeros((LANES - 16, LANES), jnp.float32)], axis=0)
        ends = jnp.transpose(ends)[skip : skip + 8]
        out[:, : depth] = own_ref[...]
        out[:, depth:] = jnp.where(lane < 16, ends, 0.0)


def sides(up, down, left, right):
    shape = (8, left.shape[1] + LANES)
    return pl.pallas_call(
        sides_kernel,
        out_shape=[jax.ShapeDtypeStruct(shape, jnp.float32)] * 2,
        compiler_params=params(4),
        name="sides",
    )(up, down, left, right)


def passes(x, inside):
    tall, wide = x.shape
    for _ in range(ITERS):
        beside = pltpu.roll(x, tall - 1, 0) + pltpu.roll(x, 1, 0) + pltpu.roll(x, wide - 1, 1) + pltpu.roll(x, 1, 1)
        x = jnp.where(inside, x + 0.2 * (beside - 4.0 * x), 0.0)
    return x


def smooth_kernel(where_ref, field_ref, up_ref, down_ref, out_ref):
    depth, width = field_ref.shape
    x = jnp.concatenate([up_ref[...], field_ref[...], down_ref[...]], axis=0)
    row = iota(x.shape, 0)
    inside = (row >= jnp.where(where_ref[0] == 0, 8, 0)) & (
        row < jnp.where(where_ref[0] == where_ref[2] - 1, 8 + depth, 16 + depth)
    )
    out_ref[...] = passes(x, inside)[8 : 8 + depth]


def smooth(where, field, up, down):
    vm = pl.BlockSpec(memory_space=pltpu.VMEM)
    return pl.pallas_call(
        smooth_kernel,
        in_specs=[pl.BlockSpec(memory_space=pltpu.SMEM)] + [vm] * 3,
        out_specs=vm,
        out_shape=jax.ShapeDtypeStruct(field.shape, jnp.float32),
        compiler_params=params(8),
        name="smooth",
    )(where, field, up, down)


def strip(where_ref, low, high, low_out, high_out):
    depth = low.shape[1] - LANES
    x = jnp.concatenate([low, high], axis=0)
    tail = x[:, depth:]
    lane = iota(tail.shape, 1)
    above = jnp.where(lane >= LANES - 8, pltpu.roll(tail, LANES - 8, 1), 0.0)
    below = jnp.where(lane < 8, pltpu.roll(tail, LANES - 8, 1), 0.0)
    x = jnp.concatenate([above, x[:, :depth], below], axis=1)
    row, col = iota(x.shape, 0), iota(x.shape, 1)
    inside = (
        (row >= jnp.where(low_out, 8, 0))
        & (row < jnp.where(high_out, 8, 16))
        & (col >= jnp.where(where_ref[0] == 0, LANES, 0))
        & (col < jnp.where(where_ref[0] == where_ref[2] - 1, LANES + depth, 2 * LANES + depth))
    )
    return passes(x, inside)[:, LANES : LANES + depth]


def grown_by(x, courant):
    keep = iota(x.shape, 1) > 0
    return x - courant * (x - jnp.where(keep, pltpu.roll(x, 1, 1), 0.0))


def grow_first_kernel(cour_ref, first_hbm, out_hbm, rows_v, out_v, sem):
    owners, ranks, _ = rows_v.shape
    load, store = copies([(first_hbm.at[:, pl.ds(0, ranks)], rows_v), (out_v, out_hbm.at[:, pl.ds(0, ranks)])], sem)
    load.start()
    load.wait()
    for o in range(owners):
        courant = sum(cour_ref[:ranks, p * owners + o : p * owners + o + 1] for p in range(3))
        out_v[o] = grown_by(rows_v[o], courant)
    store.start()
    store.wait()


def grow_first(rows, cour):
    cap, owners = cour.shape[0], rows.shape[0]
    hbm = pl.BlockSpec(memory_space=pltpu.HBM)
    return pl.pallas_call(
        grow_first_kernel,
        in_specs=[pl.BlockSpec(memory_space=pltpu.VMEM), hbm],
        out_specs=hbm,
        out_shape=jax.ShapeDtypeStruct((owners, cap, LANES), jnp.float32),
        scratch_shapes=[
            pltpu.VMEM((owners, FIRST, LANES), jnp.float32),
            pltpu.VMEM((owners, FIRST, LANES), jnp.float32),
            pltpu.SemaphoreType.DMA((2,)),
        ],
        compiler_params=params(8),
        name="grow_first",
    )(cour, rows)


def finish_kernel(
    where_ref, cour_ref, smooth_ref, left_ref, right_ref, got_left, got_right, rows_hbm, onto_hbm,
    out_hbm, field_hbm,
    rows_v, out_v, field_v, spread, sem_in, sem_out, sem_field,
):
    owners, ranks, _ = rows_v.shape
    per = owners // PARTS
    spans = [pl.ds(i * per, per) for i in range(PARTS)]
    loads = copies([(rows_hbm.at[s], rows_v.at[s]) for s in spans], sem_in)
    stores = copies([(out_v.at[s], out_hbm.at[s, pl.ds(FIRST, ranks)]) for s in spans], sem_out)
    for c in loads:
        c.start()

    depth, width = smooth_ref.shape
    zeros = jnp.zeros((LANES - 8, depth), jnp.float32)
    lane = iota((depth, LANES), 1)
    at = where_ref[1]
    west = strip(where_ref, got_left[...], left_ref[...], at == 0, False)[8:]
    east = strip(where_ref, right_ref[...], got_right[...], False, at == where_ref[3] - 1)[:8]
    west = jnp.transpose(jnp.concatenate([west, zeros], axis=0))
    east = jnp.transpose(jnp.concatenate([zeros, east], axis=0))
    if width > 2 * LANES:
        field_v[:, LANES : width - LANES] = smooth_ref[:, LANES : width - LANES]
    field_v[:, :LANES] = jnp.where(lane < ITERS, west, smooth_ref[:, :LANES])
    field_v[:, width - LANES :] = jnp.where(lane >= LANES - ITERS, east, smooth_ref[:, width - LANES :])
    store_field = pltpu.make_async_copy(field_v, field_hbm, sem_field)
    store_field.start()

    parts = cour_ref[FIRST:].astype(jnp.bfloat16)
    for i in range(PARTS):
        columns = (per * LANES, i * per)
        source = jnp.right_shift(iota((parts.shape[1], columns[0]), 1), 7) + columns[1]
        row = iota(source.shape, 0)
        picks = (jnp.bitwise_and(row, owners - 1) == source) & (row < 3 * owners)
        spread[i] = dot(parts, picks.astype(jnp.float32).astype(jnp.bfloat16), NN)

    for i in range(PARTS):
        loads[i].wait()
        for o in range(i * per, (i + 1) * per):
            begin = (o - i * per) * LANES
            out_v[o] = grown_by(rows_v[o], spread[i, :, begin : begin + LANES])
        stores[i].start()
    store_field.wait()
    for c in stores:
        c.wait()


def finish(where, cour, smoothed, left, right, got_left, got_right, rows, onto):
    hbm = pl.BlockSpec(memory_space=pltpu.HBM)
    vm = pl.BlockSpec(memory_space=pltpu.VMEM)
    return pl.pallas_call(
        finish_kernel,
        in_specs=[pl.BlockSpec(memory_space=pltpu.SMEM)] + [vm] * 6 + [hbm] * 2,
        out_specs=(hbm, hbm),
        out_shape=(
            jax.ShapeDtypeStruct(onto.shape, jnp.float32),
            jax.ShapeDtypeStruct(smoothed.shape, jnp.float32),
        ),
        scratch_shapes=[
            pltpu.VMEM(rows.shape, jnp.float32),
            pltpu.VMEM(rows.shape, jnp.float32),
            pltpu.VMEM(smoothed.shape, jnp.float32),
            pltpu.VMEM((PARTS, rows.shape[1], rows.shape[0] // PARTS * LANES), jnp.float32),
            pltpu.SemaphoreType.DMA((PARTS,)),
            pltpu.SemaphoreType.DMA((PARTS,)),
            pltpu.SemaphoreType.DMA,
        ],
        input_output_aliases={8: 0},
        compiler_params=params(24),
        name="finish",
    )(where, cour, smoothed, left, right, got_left, got_right, rows, onto)


def neighbours(low_part, high_part, axis):
    count = lax.axis_size(axis)
    forward = [(i, i + 1) for i in range(count - 1)]
    backward = [(i + 1, i) for i in range(count - 1)]
    return lax.ppermute(high_part, axis, forward), lax.ppermute(low_part, axis, backward)


def per_device(parcels, growth_rate, cell_index, dest_owner, live_count, supersat, bin_volume):
    owners = lax.axis_size("own")
    total = parcels.shape[0]
    cap = 2 * total // owners
    chunks = total // LANES
    square = lambda x: x.reshape(chunks, LANES)
    exchange = functools.partial(lax.all_to_all, axis_name="own", split_axis=0, concat_axis=0, tiled=True)
    where = jnp.stack([lax.axis_index("grp"), lax.axis_index("own"), lax.axis_size("grp"), owners]).astype(jnp.int32)
    first, src = plan(
        live_count, square(dest_owner), square(growth_rate), square(cell_index), bin_volume.reshape(1, LANES), parcels, owners, cap
    )
    got_first = exchange(first)
    rest = pack(src, parcels)
    got_rest = exchange(rest)

    field, cour, top, bottom, left, right = deposit(got_first, supersat)
    got_up, got_down = neighbours(top, bottom, "grp")
    left, right = sides(got_up, got_down, left, right)
    got_left, got_right = neighbours(left, right, "own")
    smoothed = smooth(where, field, got_up, got_down)
    onto = grow_first(got_first, cour)
    grown, field = finish(where, cour, smoothed, left, right, got_left, got_right, got_rest, onto)
    return grown.reshape(owners * cap, LANES), field


def solution(mesh):
    placed = (
        P(("grp", "own"), None),
        P(("grp", "own")),
        P(("grp", "own")),
        P(("grp", "own")),
        P(("grp", "own")),
        P("grp", "own"),
        P(),
    )
    return jax.shard_map(
        per_device,
        mesh=mesh,
        in_specs=placed,
        out_specs=(P(("grp", "own"), None), P("grp", "own")),
        check_vma=False,
    )
```

```python
import functools

import jax
import jax.numpy as jnp
from jax import lax
from jax.experimental import pallas as pl
from jax.experimental.pallas import tpu as pltpu
from jax.sharding import PartitionSpec as P

ITERS = 4
LANES = 128
FIRST = 24
BATCH = 116
META = 8
NT = (((1,), (1,)), ((), ()))
NN = (((1,), (0,)), ((), ()))
PARTS = 8


def dot(a, b, dims):
    return lax.dot_general(a, b, dims, preferred_element_type=jnp.float32)


def split3(x):
    hi = x.astype(jnp.bfloat16).astype(jnp.float32)
    rest = x - hi
    mid = rest.astype(jnp.bfloat16).astype(jnp.float32)
    return hi, mid, rest - mid


def iota(shape, dim):
    return lax.broadcasted_iota(jnp.int32, shape, dim)


def params(mib):
    return pltpu.CompilerParams(vmem_limit_bytes=mib << 20)


def copies(pairs, sems):
    return [pltpu.make_async_copy(a, b, sems.at[i]) for i, (a, b) in enumerate(pairs)]


def plan_kernel(
    live_ref, dest_hbm, rate_hbm, cell_hbm, vol_hbm, rows_hbm,
    first_hbm, src_ref,
    dest_ref, rate_ref, cell_ref, vol_ref, rows_v, first_ref, lhs, bt, vrow, src_smem, sem_in, sem_src, sem_out,
):
    chunks = dest_ref.shape[0]
    owners, cap = src_ref.shape
    total = chunks * LANES
    loads = copies(
        [
            (dest_hbm, dest_ref),
            (rows_hbm, rows_v.at[pl.ds(0, total)]),
            (vol_hbm, vol_ref),
            (rate_hbm, rate_ref),
            (cell_hbm, cell_ref),
        ],
        sem_in,
    )
    for c in loads:
        c.start()
    rows_v[total : total + 8, :] = jnp.zeros((8, LANES), jnp.float32)
    loads[0].wait()

    live = live_ref[0]
    lane = iota((1, LANES), 1)
    owner_of = iota((owners, LANES), 0)
    tri = (iota((LANES, 2 * LANES), 0) <= iota((LANES, 2 * LANES), 1)).astype(jnp.bfloat16)
    hits = []
    for s in range(chunks):
        target = jnp.where(lane + s * LANES < live, dest_ref[s : s + 1, :], -1)
        hits.append((owner_of == target).astype(jnp.float32))
    counts = dot(jnp.concatenate(hits, axis=0).astype(jnp.bfloat16), tri, NN)

    for c in loads[1:]:
        c.wait()
    vol = vol_ref[...]
    shifted = jnp.where(lane == LANES - 1, 0.0, pltpu.roll(vol, LANES - 1, 1))
    w_hi, w_mid, w_lo = split3(vol - shifted)
    weights = jnp.concatenate(
        [w_hi, w_mid, w_lo, jnp.zeros((5, LANES), jnp.float32)], axis=0
    ).astype(jnp.bfloat16)
    span = 512
    for s in range(total // span):
        r_hi, r_mid, _ = split3(rows_v[s * span : (s + 1) * span, :])
        p_hi = dot(weights, r_hi.astype(jnp.bfloat16), NT)
        p_mid = dot(weights, r_mid.astype(jnp.bfloat16), NT)
        v = p_hi[0:1] + (p_hi[1:2] + p_mid[0:1]) + (p_hi[2:3] + p_mid[1:2])
        vrow[:, s * span : (s + 1) * span] = v

    rank_of = iota((cap, LANES), 0).astype(jnp.float32)
    ranks = []
    carry = jnp.zeros((owners, LANES), jnp.float32)
    for s in range(chunks):
        hit = hits[s]
        part = counts[s * owners : (s + 1) * owners]
        rank = jnp.sum(hit * (part[:, :LANES] + carry - 1.0), axis=0, keepdims=True)
        carry = carry + part[:, LANES:]
        cols = slice(s * LANES, (s + 1) * LANES)
        ranks.append(rank)
        cell = cell_ref[s : s + 1, :]
        cell_hi = jnp.right_shift(cell + 256, 9)
        cell_lo = cell - cell_hi * 512
        values = (
            (jnp.full((1, LANES), s + 1, jnp.float32), lane.astype(jnp.float32))
            + split3(rate_ref[s : s + 1, :])[:2]
            + (cell_hi.astype(jnp.float32), cell_lo.astype(jnp.float32))
            + split3(vrow[:, cols])[:2]
        )
        for q, value in enumerate(values):
            lhs[q * owners : (q + 1) * owners, cols] = (hit * value).astype(jnp.bfloat16)

    turned = jnp.transpose(jnp.concatenate(ranks + [jnp.zeros((LANES - chunks, LANES), jnp.float32)], axis=0))
    across = iota((LANES, cap), 1).astype(jnp.float32)
    for s in range(chunks):
        bt[s * LANES : (s + 1) * LANES, :] = (across == turned[:, s : s + 1]).astype(jnp.float32).astype(jnp.bfloat16)
    packed = dot(lhs[...], bt[...], NN)
    part = [packed[q * owners : (q + 1) * owners] for q in range(8)]
    src = jnp.where(part[0] > 0.5, (part[0] - 1.0) * LANES + part[1], float(total))
    src_ref[...] = src.astype(jnp.int32)
    to_smem = pltpu.make_async_copy(src_ref, src_smem, sem_src)
    to_smem.start()
    meta = (
        part[2] + part[3],
        part[4] * 512.0 + part[5],
        part[6] + part[7],
    )
    first = first_ref.shape[1] - META
    for q, value in enumerate(meta):
        for half in range(2):
            at = first + 2 * q + half
            for j in range(owners):
                first_ref[j, at : at + 1, :] = value[j : j + 1, half * LANES : (half + 1) * LANES]
    for j in range(owners):
        first_ref[j, first + 6 : first + 8, :] = jnp.zeros((2, LANES), jnp.float32)
    to_smem.wait()

    def copy_rows(j, _):
        at = [src_smem[j, r] for r in range(first)]
        rows = [rows_v[pl.ds(i, 1), :] for i in at]
        for r in range(first):
            first_ref[j, r : r + 1, :] = rows[r]
        return 0

    per = owners // PARTS
    spans = [pl.ds(i * per, per) for i in range(PARTS)]
    stores = copies([(first_ref.at[s], first_hbm.at[s]) for s in spans], sem_out)
    for i in range(PARTS):
        lax.fori_loop(i * per, (i + 1) * per, copy_rows, 0)
        stores[i].start()
    for c in stores:
        c.wait()


def plan(live, dest, rate, cell, vol, rows, owners, cap):
    chunks = dest.shape[0]
    total = chunks * LANES
    hbm = pl.BlockSpec(memory_space=pltpu.HBM)
    return pl.pallas_call(
        plan_kernel,
        in_specs=[pl.BlockSpec(memory_space=pltpu.SMEM)] + [hbm] * 5,
        out_specs=(hbm, pl.BlockSpec(memory_space=pltpu.VMEM)),
        out_shape=(
            jax.ShapeDtypeStruct((owners, FIRST + META, LANES), jnp.float32),
            jax.ShapeDtypeStruct((owners, cap), jnp.int32),
        ),
        scratch_shapes=[
            pltpu.VMEM((chunks, LANES), jnp.int32),
            pltpu.VMEM((chunks, LANES), jnp.float32),
            pltpu.VMEM((chunks, LANES), jnp.int32),
            pltpu.VMEM((1, LANES), jnp.float32),
            pltpu.VMEM((total + 8, LANES), jnp.float32),
            pltpu.VMEM((owners, FIRST + META, LANES), jnp.float32),
            pltpu.VMEM((8 * owners, total), jnp.bfloat16),
            pltpu.VMEM((total, cap), jnp.bfloat16),
            pltpu.VMEM((1, total), jnp.float32),
            pltpu.SMEM((owners, cap), jnp.int32),
            pltpu.SemaphoreType.DMA((5,)),
            pltpu.SemaphoreType.DMA,
            pltpu.SemaphoreType.DMA((PARTS,)),
        ],
        compiler_params=params(60),
        name="plan",
    )(live, dest, rate, cell, vol, rows)


def pack_kernel(src_ref, rows_hbm, out_hbm, rows_v, out_v, sem_rows, sem_out):
    total = rows_v.shape[0] - 8
    owners, ranks, _ = out_v.shape
    load = pltpu.make_async_copy(rows_hbm, rows_v.at[pl.ds(0, total)], sem_rows)
    load.start()
    rows_v[total : total + 8, :] = jnp.zeros((8, LANES), jnp.float32)

    def clear(j, _):
        out_v[j] = jnp.zeros((ranks, LANES), jnp.float32)
        return 0

    lax.fori_loop(0, owners, clear, 0)
    load.wait()
    per = owners // PARTS
    spans = [pl.ds(i * per, per) for i in range(PARTS)]
    stores = copies([(out_v.at[s], out_hbm.at[s]) for s in spans], sem_out)

    def copy_rows(j, _):
        for base in range(0, ranks, BATCH):
            @pl.when(src_ref[j, FIRST + base] < total)
            def _():
                at = [src_ref[j, FIRST + base + r] for r in range(BATCH)]
                rows = [rows_v[pl.ds(i, 1), :] for i in at]
                for r in range(BATCH):
                    out_v[j, base + r : base + r + 1, :] = rows[r]

        return 0

    for i in range(PARTS):
        lax.fori_loop(i * per, (i + 1) * per, copy_rows, 0)
        stores[i].start()
    for c in stores:
        c.wait()


def pack(src, rows):
    owners, cap = src.shape
    total = rows.shape[0]
    hbm = pl.BlockSpec(memory_space=pltpu.HBM)
    shape = (owners, cap - FIRST, LANES)
    return pl.pallas_call(
        pack_kernel,
        in_specs=[pl.BlockSpec(memory_space=pltpu.SMEM), hbm],
        out_specs=hbm,
        out_shape=jax.ShapeDtypeStruct(shape, jnp.float32),
        scratch_shapes=[
            pltpu.VMEM((total + 8, LANES), jnp.float32),
            pltpu.VMEM(shape, jnp.float32),
            pltpu.SemaphoreType.DMA,
            pltpu.SemaphoreType.DMA((PARTS,)),
        ],
        compiler_params=params(60),
        cost_estimate=pl.CostEstimate(flops=0, bytes_accessed=24 << 20, transcendentals=0),
        name="pack",
    )(src, rows)


def deposit_kernel(
    first_hbm, sup_hbm, field_ref, cour_ref, top_ref, bottom_ref, left_ref, right_ref,
    meta_ref, sup_ref, table, high, acc, cour, sem,
):
    depth, width = sup_ref.shape
    owners = meta_ref.shape[0]
    loads = copies([(sup_hbm, sup_ref), (first_hbm.at[:, pl.ds(FIRST, META)], meta_ref)], sem)
    for c in loads:
        c.start()
    for c in loads:
        c.wait()
    group = 4
    n = group * 2 * LANES
    flipped = jnp.transpose(sup_ref[...])
    f_hi = flipped.astype(jnp.bfloat16)
    table[:width, :] = f_hi
    table[width:, :] = (flipped - f_hi.astype(jnp.float32)).astype(jnp.bfloat16)
    acc[...] = jnp.zeros_like(acc)

    def step(g, _):
        def lane_row(q):
            return jnp.concatenate(
                [meta_ref[g * group + o, 2 * q + half : 2 * q + half + 1, :] for o in range(group) for half in range(2)],
                axis=1,
            )

        rate, cell, v = lane_row(0), lane_row(1).astype(jnp.int32), lane_row(2)
        row_at = jnp.right_shift(cell, 8)
        col_at = jnp.bitwise_and(cell, 255)
        high[...] = (iota((depth, n), 0) == row_at).astype(jnp.float32).astype(jnp.bfloat16)
        lines = dot(table[...], high[...], NN)
        across = iota((width, n), 0) == col_at
        sat = jnp.sum(jnp.where(across, lines[:width] + lines[width:], 0.0), axis=0, keepdims=True)
        courant = rate * sat
        for o in range(group):
            cour[pl.ds(g * group + o, 1), :] = courant[:, o * 2 * LANES : (o + 1) * 2 * LANES]
        mass = courant * v
        m_hi = mass.astype(jnp.bfloat16).astype(jnp.float32)
        spread = jnp.concatenate(
            [jnp.where(across, m_hi, 0.0).astype(jnp.bfloat16), jnp.where(across, mass - m_hi, 0.0).astype(jnp.bfloat16)],
            axis=0,
        )
        acc[...] += dot(high[...], spread, NT)
        return 0

    lax.fori_loop(0, owners // group, step, 0)
    field = sup_ref[...] - 0.5 * (acc[:, :width] + acc[:, width:])
    field_ref[...] = field
    cour_ref[...] = jnp.transpose(jnp.concatenate(split3(cour[...]) + (jnp.zeros_like(cour),), axis=0))
    top_ref[...] = field[:8]
    bottom_ref[...] = field[depth - 8 :]
    left_ref[...] = jnp.transpose(field[:, :LANES])[:8]
    right_ref[...] = jnp.transpose(field[:, width - LANES :])[LANES - 8 :]


def deposit(got_first, supersat):
    owners = got_first.shape[0]
    depth, width = supersat.shape
    f32 = jnp.float32
    vm = pl.BlockSpec(memory_space=pltpu.VMEM)
    hbm = pl.BlockSpec(memory_space=pltpu.HBM)
    outs = [(depth, width), (2 * LANES, 4 * owners), (8, width), (8, width), (8, depth), (8, depth)]
    return pl.pallas_call(
        deposit_kernel,
        in_specs=[hbm, hbm],
        out_specs=[vm] * len(outs),
        out_shape=[jax.ShapeDtypeStruct(s, f32) for s in outs],
        scratch_shapes=[
            pltpu.VMEM((owners, META, LANES), f32),
            pltpu.VMEM((depth, width), f32),
            pltpu.VMEM((2 * width, depth), jnp.bfloat16),
            pltpu.VMEM((depth, 8 * LANES), jnp.bfloat16),
            pltpu.VMEM((depth, 2 * width), f32),
            pltpu.VMEM((owners, 2 * LANES), f32),
            pltpu.SemaphoreType.DMA((2,)),
        ],
        compiler_params=params(16),
        cost_estimate=pl.CostEstimate(flops=9 << 30, bytes_accessed=8 << 20, transcendentals=0),
        name="deposit",
    )(got_first, supersat)


def sides_kernel(up_ref, down_ref, left_ref, right_ref, out_left, out_right):
    depth = left_ref.shape[1]
    width = up_ref.shape[1]
    lane = iota((8, LANES), 1)
    for out, own_ref, begin in ((out_left, left_ref, 0), (out_right, right_ref, width - LANES)):
        skip = 0 if begin == 0 else LANES - 8
        ends = jnp.concatenate([up_ref[:, begin : begin + LANES], down_ref[:, begin : begin + LANES]], axis=0)
        ends = jnp.concatenate([ends, jnp.zeros((LANES - 16, LANES), jnp.float32)], axis=0)
        ends = jnp.transpose(ends)[skip : skip + 8]
        out[:, : depth] = own_ref[...]
        out[:, depth:] = jnp.where(lane < 16, ends, 0.0)


def sides(up, down, left, right):
    shape = (8, left.shape[1] + LANES)
    return pl.pallas_call(
        sides_kernel,
        out_shape=[jax.ShapeDtypeStruct(shape, jnp.float32)] * 2,
        compiler_params=params(4),
        name="sides",
    )(up, down, left, right)


def passes(x, inside):
    tall, wide = x.shape
    for _ in range(ITERS):
        beside = pltpu.roll(x, tall - 1, 0) + pltpu.roll(x, 1, 0) + pltpu.roll(x, wide - 1, 1) + pltpu.roll(x, 1, 1)
        x = jnp.where(inside, x + 0.2 * (beside - 4.0 * x), 0.0)
    return x


def smooth_kernel(where_ref, field_ref, up_ref, down_ref, out_ref):
    depth, width = field_ref.shape
    x = jnp.concatenate([up_ref[...], field_ref[...], down_ref[...]], axis=0)
    row = iota(x.shape, 0)
    inside = (row >= jnp.where(where_ref[0] == 0, 8, 0)) & (
        row < jnp.where(where_ref[0] == where_ref[2] - 1, 8 + depth, 16 + depth)
    )
    out_ref[...] = passes(x, inside)[8 : 8 + depth]


def smooth(where, field, up, down):
    vm = pl.BlockSpec(memory_space=pltpu.VMEM)
    return pl.pallas_call(
        smooth_kernel,
        in_specs=[pl.BlockSpec(memory_space=pltpu.SMEM)] + [vm] * 3,
        out_specs=vm,
        out_shape=jax.ShapeDtypeStruct(field.shape, jnp.float32),
        compiler_params=params(8),
        name="smooth",
    )(where, field, up, down)


def strip(where_ref, low, high, low_out, high_out):
    depth = low.shape[1] - LANES
    x = jnp.concatenate([low, high], axis=0)
    tail = x[:, depth:]
    lane = iota(tail.shape, 1)
    above = jnp.where(lane >= LANES - 8, pltpu.roll(tail, LANES - 8, 1), 0.0)
    below = jnp.where(lane < 8, pltpu.roll(tail, LANES - 8, 1), 0.0)
    x = jnp.concatenate([above, x[:, :depth], below], axis=1)
    row, col = iota(x.shape, 0), iota(x.shape, 1)
    inside = (
        (row >= jnp.where(low_out, 8, 0))
        & (row < jnp.where(high_out, 8, 16))
        & (col >= jnp.where(where_ref[0] == 0, LANES, 0))
        & (col < jnp.where(where_ref[0] == where_ref[2] - 1, LANES + depth, 2 * LANES + depth))
    )
    return passes(x, inside)[:, LANES : LANES + depth]


def grown_by(x, courant):
    keep = iota(x.shape, 1) > 0
    return x - courant * (x - jnp.where(keep, pltpu.roll(x, 1, 1), 0.0))


def grow_first_kernel(cour_ref, first_hbm, out_hbm, rows_v, out_v, sem):
    owners, ranks, _ = rows_v.shape
    load, store = copies([(first_hbm.at[:, pl.ds(0, ranks)], rows_v), (out_v, out_hbm.at[:, pl.ds(0, ranks)])], sem)
    load.start()
    load.wait()
    for o in range(owners):
        courant = sum(cour_ref[:ranks, p * owners + o : p * owners + o + 1] for p in range(3))
        out_v[o] = grown_by(rows_v[o], courant)
    store.start()
    store.wait()


def grow_first(rows, cour):
    cap, owners = cour.shape[0], rows.shape[0]
    hbm = pl.BlockSpec(memory_space=pltpu.HBM)
    return pl.pallas_call(
        grow_first_kernel,
        in_specs=[pl.BlockSpec(memory_space=pltpu.VMEM), hbm],
        out_specs=hbm,
        out_shape=jax.ShapeDtypeStruct((owners, cap, LANES), jnp.float32),
        scratch_shapes=[
            pltpu.VMEM((owners, FIRST, LANES), jnp.float32),
            pltpu.VMEM((owners, FIRST, LANES), jnp.float32),
            pltpu.SemaphoreType.DMA((2,)),
        ],
        compiler_params=params(8),
        name="grow_first",
    )(cour, rows)


def finish_kernel(
    where_ref, cour_ref, smooth_ref, left_ref, right_ref, got_left, got_right, rows_hbm, onto_hbm,
    out_hbm, field_hbm,
    rows_v, out_v, field_v, spread, sem_in, sem_out, sem_field,
):
    owners, ranks, _ = rows_v.shape
    per = owners // PARTS
    spans = [pl.ds(i * per, per) for i in range(PARTS)]
    loads = copies([(rows_hbm.at[s], rows_v.at[s]) for s in spans], sem_in)
    stores = copies([(out_v.at[s], out_hbm.at[s, pl.ds(FIRST, ranks)]) for s in spans], sem_out)
    for c in loads:
        c.start()

    depth, width = smooth_ref.shape
    zeros = jnp.zeros((LANES - 8, depth), jnp.float32)
    lane = iota((depth, LANES), 1)
    at = where_ref[1]
    west = strip(where_ref, got_left[...], left_ref[...], at == 0, False)[8:]
    east = strip(where_ref, right_ref[...], got_right[...], False, at == where_ref[3] - 1)[:8]
    west = jnp.transpose(jnp.concatenate([west, zeros], axis=0))
    east = jnp.transpose(jnp.concatenate([zeros, east], axis=0))
    if width > 2 * LANES:
        field_v[:, LANES : width - LANES] = smooth_ref[:, LANES : width - LANES]
    field_v[:, :LANES] = jnp.where(lane < ITERS, west, smooth_ref[:, :LANES])
    field_v[:, width - LANES :] = jnp.where(lane >= LANES - ITERS, east, smooth_ref[:, width - LANES :])
    store_field = pltpu.make_async_copy(field_v, field_hbm, sem_field)
    store_field.start()

    parts = cour_ref[FIRST:].astype(jnp.bfloat16)
    for i in range(PARTS):
        columns = (per * LANES, i * per)
        source = jnp.right_shift(iota((parts.shape[1], columns[0]), 1), 7) + columns[1]
        row = iota(source.shape, 0)
        picks = (jnp.bitwise_and(row, owners - 1) == source) & (row < 3 * owners)
        spread[i] = dot(parts, picks.astype(jnp.float32).astype(jnp.bfloat16), NN)

    for i in range(PARTS):
        loads[i].wait()
        for o in range(i * per, (i + 1) * per):
            begin = (o - i * per) * LANES
            out_v[o] = grown_by(rows_v[o], spread[i, :, begin : begin + LANES])
        stores[i].start()
    store_field.wait()
    for c in stores:
        c.wait()


def finish(where, cour, smoothed, left, right, got_left, got_right, rows, onto):
    hbm = pl.BlockSpec(memory_space=pltpu.HBM)
    vm = pl.BlockSpec(memory_space=pltpu.VMEM)
    return pl.pallas_call(
        finish_kernel,
        in_specs=[pl.BlockSpec(memory_space=pltpu.SMEM)] + [vm] * 6 + [hbm] * 2,
        out_specs=(hbm, hbm),
        out_shape=(
            jax.ShapeDtypeStruct(onto.shape, jnp.float32),
            jax.ShapeDtypeStruct(smoothed.shape, jnp.float32),
        ),
        scratch_shapes=[
            pltpu.VMEM(rows.shape, jnp.float32),
            pltpu.VMEM(rows.shape, jnp.float32),
            pltpu.VMEM(smoothed.shape, jnp.float32),
            pltpu.VMEM((PARTS, rows.shape[1], rows.shape[0] // PARTS * LANES), jnp.float32),
            pltpu.SemaphoreType.DMA((PARTS,)),
            pltpu.SemaphoreType.DMA((PARTS,)),
            pltpu.SemaphoreType.DMA,
        ],
        input_output_aliases={8: 0},
        compiler_params=params(24),
        name="finish",
    )(where, cour, smoothed, left, right, got_left, got_right, rows, onto)


def neighbours(low_part, high_part, axis):
    count = lax.axis_size(axis)
    forward = [(i, i + 1) for i in range(count - 1)]
    backward = [(i + 1, i) for i in range(count - 1)]
    return lax.ppermute(high_part, axis, forward), lax.ppermute(low_part, axis, backward)


def per_device(parcels, growth_rate, cell_index, dest_owner, live_count, supersat, bin_volume):
    owners = lax.axis_size("own")
    total = parcels.shape[0]
    cap = 2 * total // owners
    chunks = total // LANES
    square = lambda x: x.reshape(chunks, LANES)
    exchange = functools.partial(lax.all_to_all, axis_name="own", split_axis=0, concat_axis=0, tiled=True)
    where = jnp.stack([lax.axis_index("grp"), lax.axis_index("own"), lax.axis_size("grp"), owners]).astype(jnp.int32)
    first, src = plan(
        live_count, square(dest_owner), square(growth_rate), square(cell_index), bin_volume.reshape(1, LANES), parcels, owners, cap
    )
    got_first = exchange(first)
    rest = pack(src, parcels)
    got_rest = exchange(rest)

    field, cour, top, bottom, left, right = deposit(got_first, supersat)
    got_up, got_down = neighbours(top, bottom, "grp")
    left, right = sides(got_up, got_down, left, right)
    got_left, got_right = neighbours(left, right, "own")
    smoothed = smooth(where, field, got_up, got_down)
    onto = grow_first(got_first, cour)
    grown, field = finish(where, cour, smoothed, left, right, got_left, got_right, got_rest, onto)
    return grown.reshape(owners * cap, LANES), field


def solution(mesh):
    placed = (
        P(("grp", "own"), None),
        P(("grp", "own")),
        P(("grp", "own")),
        P(("grp", "own")),
        P(("grp", "own")),
        P("grp", "own"),
        P(),
    )
    return jax.shard_map(
        per_device,
        mesh=mesh,
        in_specs=placed,
        out_specs=(P(("grp", "own"), None), P("grp", "own")),
        check_vma=False,
    )
```

```python
import functools

import jax
import jax.numpy as jnp
from jax import lax
from jax.experimental import pallas as pl
from jax.experimental.pallas import tpu as pltpu
from jax.sharding import PartitionSpec as P

ITERS = 4
LANES = 128
FIRST = 32
BATCH = 112
META = 8
NT = (((1,), (1,)), ((), ()))
NN = (((1,), (0,)), ((), ()))
PARTS = 8


def dot(a, b, dims):
    return lax.dot_general(a, b, dims, preferred_element_type=jnp.float32)


def split3(x):
    hi = x.astype(jnp.bfloat16).astype(jnp.float32)
    rest = x - hi
    mid = rest.astype(jnp.bfloat16).astype(jnp.float32)
    return hi, mid, rest - mid


def iota(shape, dim):
    return lax.broadcasted_iota(jnp.int32, shape, dim)


def params(mib):
    return pltpu.CompilerParams(vmem_limit_bytes=mib << 20)


def copies(pairs, sems):
    return [pltpu.make_async_copy(a, b, sems.at[i]) for i, (a, b) in enumerate(pairs)]


def plan_kernel(
    live_ref, dest_hbm, rate_hbm, cell_hbm, vol_hbm, rows_hbm,
    first_hbm, src_ref,
    dest_ref, rate_ref, cell_ref, vol_ref, rows_v, first_ref, lhs, bt, vrow, src_smem, sem_in, sem_src, sem_out,
):
    chunks = dest_ref.shape[0]
    owners, cap = src_ref.shape
    total = chunks * LANES
    loads = copies(
        [
            (dest_hbm, dest_ref),
            *[(rows_hbm.at[pl.ds(i * total // 4, total // 4)], rows_v.at[pl.ds(i * total // 4, total // 4)]) for i in range(4)],
            (vol_hbm, vol_ref),
            (rate_hbm, rate_ref),
            (cell_hbm, cell_ref),
        ],
        sem_in,
    )
    for c in loads:
        c.start()
    rows_v[total : total + 8, :] = jnp.zeros((8, LANES), jnp.float32)
    loads[0].wait()

    live = live_ref[0]
    lane = iota((1, LANES), 1)
    owner_of = iota((owners, LANES), 0)
    tri = (iota((LANES, 2 * LANES), 0) <= iota((LANES, 2 * LANES), 1)).astype(jnp.bfloat16)
    hits = []
    for s in range(chunks):
        target = jnp.where(lane + s * LANES < live, dest_ref[s : s + 1, :], -1)
        hits.append((owner_of == target).astype(jnp.float32))
    counts = dot(jnp.concatenate(hits, axis=0).astype(jnp.bfloat16), tri, NN)

    for c in loads[1:]:
        c.wait()
    vol = vol_ref[...]
    shifted = jnp.where(lane == LANES - 1, 0.0, pltpu.roll(vol, LANES - 1, 1))
    w_hi, w_mid, w_lo = split3(vol - shifted)
    weights = jnp.concatenate(
        [w_hi, w_mid, w_lo, jnp.zeros((5, LANES), jnp.float32)], axis=0
    ).astype(jnp.bfloat16)
    span = 512
    for s in range(total // span):
        r_hi, r_mid, _ = split3(rows_v[s * span : (s + 1) * span, :])
        p_hi = dot(weights, r_hi.astype(jnp.bfloat16), NT)
        p_mid = dot(weights, r_mid.astype(jnp.bfloat16), NT)
        v = p_hi[0:1] + (p_hi[1:2] + p_mid[0:1]) + (p_hi[2:3] + p_mid[1:2])
        vrow[:, s * span : (s + 1) * span] = v

    rank_of = iota((cap, LANES), 0).astype(jnp.float32)
    ranks = []
    carry = jnp.zeros((owners, LANES), jnp.float32)
    for s in range(chunks):
        hit = hits[s]
        packed_hit = hit.astype(jnp.bfloat16)
        part = counts[s * owners : (s + 1) * owners]
        rank = jnp.sum(hit * (part[:, :LANES] + carry - 1.0), axis=0, keepdims=True)
        carry = carry + part[:, LANES:]
        cols = slice(s * LANES, (s + 1) * LANES)
        ranks.append(rank)
        cell = cell_ref[s : s + 1, :]
        cell_hi = jnp.right_shift(cell + 256, 9)
        cell_lo = cell - cell_hi * 512
        values = (
            (jnp.full((1, LANES), s + 1, jnp.float32), lane.astype(jnp.float32))
            + split3(rate_ref[s : s + 1, :])[:2]
            + (cell_hi.astype(jnp.float32), cell_lo.astype(jnp.float32))
            + split3(vrow[:, cols])[:2]
        )
        for q, value in enumerate(values):
            lhs[q * owners : (q + 1) * owners, cols] = packed_hit * value.astype(jnp.bfloat16)

    turned = jnp.transpose(jnp.concatenate(ranks + [jnp.zeros((LANES - chunks, LANES), jnp.float32)], axis=0))
    across = iota((LANES, cap), 1).astype(jnp.float32)
    for s in range(chunks):
        bt[s * LANES : (s + 1) * LANES, :] = (across == turned[:, s : s + 1]).astype(jnp.float32).astype(jnp.bfloat16)
    packed = dot(lhs[...], bt[...], NN)
    part = [packed[q * owners : (q + 1) * owners] for q in range(8)]
    src = jnp.where(part[0] > 0.5, (part[0] - 1.0) * LANES + part[1], float(total))
    src_ref[...] = src.astype(jnp.int32)
    to_smem = pltpu.make_async_copy(src_ref, src_smem, sem_src)
    to_smem.start()
    meta = (
        part[2] + part[3],
        part[4] * 512.0 + part[5],
        part[6] + part[7],
    )
    first = first_ref.shape[1] - META
    for q, value in enumerate(meta):
        for half in range(2):
            at = first + 2 * q + half
            for j in range(owners):
                first_ref[j, at : at + 1, :] = value[j : j + 1, half * LANES : (half + 1) * LANES]
    for j in range(owners):
        first_ref[j, first + 6 : first + 8, :] = jnp.zeros((2, LANES), jnp.float32)
    to_smem.wait()

    def copy_rows(j, _):
        at = [src_smem[j, r] for r in range(first)]
        rows = [rows_v[pl.ds(i, 1), :] for i in at]
        for r in range(first):
            first_ref[j, r : r + 1, :] = rows[r]
        return 0

    per = owners // PARTS
    spans = [pl.ds(i * per, per) for i in range(PARTS)]
    stores = copies([(first_ref.at[s], first_hbm.at[s]) for s in spans], sem_out)
    for i in range(PARTS):
        lax.fori_loop(i * per, (i + 1) * per, copy_rows, 0)
        stores[i].start()
    for c in stores:
        c.wait()


def plan(live, dest, rate, cell, vol, rows, owners, cap):
    chunks = dest.shape[0]
    total = chunks * LANES
    hbm = pl.BlockSpec(memory_space=pltpu.HBM)
    return pl.pallas_call(
        plan_kernel,
        in_specs=[pl.BlockSpec(memory_space=pltpu.SMEM)] + [hbm] * 5,
        out_specs=(hbm, pl.BlockSpec(memory_space=pltpu.VMEM)),
        out_shape=(
            jax.ShapeDtypeStruct((owners, FIRST + META, LANES), jnp.float32),
            jax.ShapeDtypeStruct((owners, cap), jnp.int32),
        ),
        scratch_shapes=[
            pltpu.VMEM((chunks, LANES), jnp.int32),
            pltpu.VMEM((chunks, LANES), jnp.float32),
            pltpu.VMEM((chunks, LANES), jnp.int32),
            pltpu.VMEM((1, LANES), jnp.float32),
            pltpu.VMEM((total + 8, LANES), jnp.float32),
            pltpu.VMEM((owners, FIRST + META, LANES), jnp.float32),
            pltpu.VMEM((8 * owners, total), jnp.bfloat16),
            pltpu.VMEM((total, cap), jnp.bfloat16),
            pltpu.VMEM((1, total), jnp.float32),
            pltpu.SMEM((owners, cap), jnp.int32),
            pltpu.SemaphoreType.DMA((8,)),
            pltpu.SemaphoreType.DMA,
            pltpu.SemaphoreType.DMA((PARTS,)),
        ],
        compiler_params=params(60),
        name="plan",
    )(live, dest, rate, cell, vol, rows)


def pack_kernel(src_ref, rows_hbm, out_hbm, rows_v, out_v, sem_rows, sem_out):
    total = rows_v.shape[0] - 8
    owners, ranks, _ = out_v.shape
    load = pltpu.make_async_copy(rows_hbm, rows_v.at[pl.ds(0, total)], sem_rows)
    load.start()
    rows_v[total : total + 8, :] = jnp.zeros((8, LANES), jnp.float32)

    def clear(j, _):
        out_v[j] = jnp.zeros((ranks, LANES), jnp.float32)
        return 0

    lax.fori_loop(0, owners, clear, 0)
    load.wait()
    per = owners // PARTS
    spans = [pl.ds(i * per, per) for i in range(PARTS)]
    stores = copies([(out_v.at[s], out_hbm.at[s]) for s in spans], sem_out)

    def copy_rows(j, _):
        for base in range(0, ranks, BATCH):
            @pl.when(src_ref[j, FIRST + base] < total)
            def _():
                at = [src_ref[j, FIRST + base + r] for r in range(BATCH)]
                rows = [rows_v[pl.ds(i, 1), :] for i in at]
                for r in range(BATCH):
                    out_v[j, base + r : base + r + 1, :] = rows[r]

        return 0

    for i in range(PARTS):
        lax.fori_loop(i * per, (i + 1) * per, copy_rows, 0)
        stores[i].start()
    for c in stores:
        c.wait()


def pack(src, rows):
    owners, cap = src.shape
    total = rows.shape[0]
    hbm = pl.BlockSpec(memory_space=pltpu.HBM)
    shape = (owners, cap - FIRST, LANES)
    return pl.pallas_call(
        pack_kernel,
        in_specs=[pl.BlockSpec(memory_space=pltpu.SMEM), hbm],
        out_specs=hbm,
        out_shape=jax.ShapeDtypeStruct(shape, jnp.float32),
        scratch_shapes=[
            pltpu.VMEM((total + 8, LANES), jnp.float32),
            pltpu.VMEM(shape, jnp.float32),
            pltpu.SemaphoreType.DMA,
            pltpu.SemaphoreType.DMA((PARTS,)),
        ],
        compiler_params=params(60),
        cost_estimate=pl.CostEstimate(flops=0, bytes_accessed=24 << 20, transcendentals=0),
        name="pack",
    )(src, rows)


def deposit_kernel(
    first_hbm, sup_hbm, field_ref, cour_ref, top_ref, bottom_ref, left_ref, right_ref,
    meta_ref, sup_ref, table, high, acc, cour, sem,
):
    depth, width = sup_ref.shape
    owners = meta_ref.shape[0]
    loads = copies([(sup_hbm, sup_ref), (first_hbm.at[:, pl.ds(FIRST, META)], meta_ref)], sem)
    for c in loads:
        c.start()
    for c in loads:
        c.wait()
    group = 4
    n = group * 2 * LANES
    flipped = jnp.transpose(sup_ref[...])
    f_hi = flipped.astype(jnp.bfloat16)
    table[:width, :] = f_hi
    table[width:, :] = (flipped - f_hi.astype(jnp.float32)).astype(jnp.bfloat16)
    acc[...] = jnp.zeros_like(acc)

    def step(g, _):
        def lane_row(q):
            return jnp.concatenate(
                [meta_ref[g * group + o, 2 * q + half : 2 * q + half + 1, :] for o in range(group) for half in range(2)],
                axis=1,
            )

        rate, cell, v = lane_row(0), lane_row(1).astype(jnp.int32), lane_row(2)
        row_at = jnp.right_shift(cell, 8)
        col_at = jnp.bitwise_and(cell, 255)
        high[...] = (iota((depth, n), 0) == row_at).astype(jnp.float32).astype(jnp.bfloat16)
        lines = dot(table[...], high[...], NN)
        across = iota((width, n), 0) == col_at
        sat = jnp.sum(jnp.where(across, lines[:width] + lines[width:], 0.0), axis=0, keepdims=True)
        courant = rate * sat
        for o in range(group):
            cour[pl.ds(g * group + o, 1), :] = courant[:, o * 2 * LANES : (o + 1) * 2 * LANES]
        mass = courant * v
        m_hi = mass.astype(jnp.bfloat16).astype(jnp.float32)
        spread = jnp.concatenate(
            [jnp.where(across, m_hi, 0.0).astype(jnp.bfloat16), jnp.where(across, mass - m_hi, 0.0).astype(jnp.bfloat16)],
            axis=0,
        )
        acc[...] += dot(high[...], spread, NT)
        return 0

    lax.fori_loop(0, owners // group, step, 0)
    field = sup_ref[...] - 0.5 * (acc[:, :width] + acc[:, width:])
    field_ref[...] = field
    cour_ref[...] = jnp.transpose(jnp.concatenate(split3(cour[...]) + (jnp.zeros_like(cour),), axis=0))
    top_ref[...] = field[:8]
    bottom_ref[...] = field[depth - 8 :]
    left_ref[...] = jnp.transpose(field[:, :LANES])[:8]
    right_ref[...] = jnp.transpose(field[:, width - LANES :])[LANES - 8 :]


def deposit(got_first, supersat):
    owners = got_first.shape[0]
    depth, width = supersat.shape
    f32 = jnp.float32
    vm = pl.BlockSpec(memory_space=pltpu.VMEM)
    hbm = pl.BlockSpec(memory_space=pltpu.HBM)
    outs = [(depth, width), (2 * LANES, 4 * owners), (8, width), (8, width), (8, depth), (8, depth)]
    return pl.pallas_call(
        deposit_kernel,
        in_specs=[hbm, hbm],
        out_specs=[vm] * len(outs),
        out_shape=[jax.ShapeDtypeStruct(s, f32) for s in outs],
        scratch_shapes=[
            pltpu.VMEM((owners, META, LANES), f32),
            pltpu.VMEM((depth, width), f32),
            pltpu.VMEM((2 * width, depth), jnp.bfloat16),
            pltpu.VMEM((depth, 8 * LANES), jnp.bfloat16),
            pltpu.VMEM((depth, 2 * width), f32),
            pltpu.VMEM((owners, 2 * LANES), f32),
            pltpu.SemaphoreType.DMA((2,)),
        ],
        compiler_params=params(16),
        cost_estimate=pl.CostEstimate(flops=9 << 30, bytes_accessed=8 << 20, transcendentals=0),
        name="deposit",
    )(got_first, supersat)


def sides_kernel(up_ref, down_ref, left_ref, right_ref, out_left, out_right):
    depth = left_ref.shape[1]
    width = up_ref.shape[1]
    lane = iota((8, LANES), 1)
    for out, own_ref, begin in ((out_left, left_ref, 0), (out_right, right_ref, width - LANES)):
        skip = 0 if begin == 0 else LANES - 8
        ends = jnp.concatenate([up_ref[:, begin : begin + LANES], down_ref[:, begin : begin + LANES]], axis=0)
        ends = jnp.concatenate([ends, jnp.zeros((LANES - 16, LANES), jnp.float32)], axis=0)
        ends = jnp.transpose(ends)[skip : skip + 8]
        out[:, : depth] = own_ref[...]
        out[:, depth:] = jnp.where(lane < 16, ends, 0.0)


def sides(up, down, left, right):
    shape = (8, left.shape[1] + LANES)
    return pl.pallas_call(
        sides_kernel,
        out_shape=[jax.ShapeDtypeStruct(shape, jnp.float32)] * 2,
        compiler_params=params(4),
        name="sides",
    )(up, down, left, right)


def passes(x, inside):
    tall, wide = x.shape
    for _ in range(ITERS):
        beside = pltpu.roll(x, tall - 1, 0) + pltpu.roll(x, 1, 0) + pltpu.roll(x, wide - 1, 1) + pltpu.roll(x, 1, 1)
        x = jnp.where(inside, x + 0.2 * (beside - 4.0 * x), 0.0)
    return x


def smooth_kernel(where_ref, field_ref, up_ref, down_ref, out_ref):
    depth, width = field_ref.shape
    x = jnp.concatenate([up_ref[...], field_ref[...], down_ref[...]], axis=0)
    row = iota(x.shape, 0)
    inside = (row >= jnp.where(where_ref[0] == 0, 8, 0)) & (
        row < jnp.where(where_ref[0] == where_ref[2] - 1, 8 + depth, 16 + depth)
    )
    out_ref[...] = passes(x, inside)[8 : 8 + depth]


def smooth(where, field, up, down):
    vm = pl.BlockSpec(memory_space=pltpu.VMEM)
    return pl.pallas_call(
        smooth_kernel,
        in_specs=[pl.BlockSpec(memory_space=pltpu.SMEM)] + [vm] * 3,
        out_specs=vm,
        out_shape=jax.ShapeDtypeStruct(field.shape, jnp.float32),
        compiler_params=params(8),
        name="smooth",
    )(where, field, up, down)


def strip(where_ref, low, high, low_out, high_out):
    depth = low.shape[1] - LANES
    x = jnp.concatenate([low, high], axis=0)
    tail = x[:, depth:]
    lane = iota(tail.shape, 1)
    above = jnp.where(lane >= LANES - 8, pltpu.roll(tail, LANES - 8, 1), 0.0)
    below = jnp.where(lane < 8, pltpu.roll(tail, LANES - 8, 1), 0.0)
    x = jnp.concatenate([above, x[:, :depth], below], axis=1)
    row, col = iota(x.shape, 0), iota(x.shape, 1)
    inside = (
        (row >= jnp.where(low_out, 8, 0))
        & (row < jnp.where(high_out, 8, 16))
        & (col >= jnp.where(where_ref[0] == 0, LANES, 0))
        & (col < jnp.where(where_ref[0] == where_ref[2] - 1, LANES + depth, 2 * LANES + depth))
    )
    return passes(x, inside)[:, LANES : LANES + depth]


def grown_by(x, courant):
    keep = iota(x.shape, 1) > 0
    return x - courant * (x - jnp.where(keep, pltpu.roll(x, 1, 1), 0.0))


def grow_first_kernel(cour_ref, first_hbm, out_hbm, rows_v, out_v, sem):
    owners, ranks, _ = rows_v.shape
    load, store = copies([(first_hbm.at[:, pl.ds(0, ranks)], rows_v), (out_v, out_hbm.at[:, pl.ds(0, ranks)])], sem)
    load.start()
    load.wait()
    for o in range(owners):
        courant = sum(cour_ref[:ranks, p * owners + o : p * owners + o + 1] for p in range(3))
        out_v[o] = grown_by(rows_v[o], courant)
    store.start()
    store.wait()


def grow_first(rows, cour):
    cap, owners = cour.shape[0], rows.shape[0]
    hbm = pl.BlockSpec(memory_space=pltpu.HBM)
    return pl.pallas_call(
        grow_first_kernel,
        in_specs=[pl.BlockSpec(memory_space=pltpu.VMEM), hbm],
        out_specs=hbm,
        out_shape=jax.ShapeDtypeStruct((owners, cap, LANES), jnp.float32),
        scratch_shapes=[
            pltpu.VMEM((owners, FIRST, LANES), jnp.float32),
            pltpu.VMEM((owners, FIRST, LANES), jnp.float32),
            pltpu.SemaphoreType.DMA((2,)),
        ],
        compiler_params=params(8),
        name="grow_first",
    )(cour, rows)


def finish_kernel(
    where_ref, cour_ref, smooth_ref, left_ref, right_ref, got_left, got_right, rows_hbm, onto_hbm,
    out_hbm, field_hbm,
    rows_v, out_v, field_v, spread, sem_in, sem_out, sem_field,
):
    owners, ranks, _ = rows_v.shape
    per = owners // PARTS
    spans = [pl.ds(i * per, per) for i in range(PARTS)]
    loads = copies([(rows_hbm.at[s], rows_v.at[s]) for s in spans], sem_in)
    stores = copies([(out_v.at[s], out_hbm.at[s, pl.ds(FIRST, ranks)]) for s in spans], sem_out)
    for c in loads:
        c.start()

    depth, width = smooth_ref.shape
    zeros = jnp.zeros((LANES - 8, depth), jnp.float32)
    lane = iota((depth, LANES), 1)
    at = where_ref[1]
    west = strip(where_ref, got_left[...], left_ref[...], at == 0, False)[8:]
    east = strip(where_ref, right_ref[...], got_right[...], False, at == where_ref[3] - 1)[:8]
    west = jnp.transpose(jnp.concatenate([west, zeros], axis=0))
    east = jnp.transpose(jnp.concatenate([zeros, east], axis=0))
    if width > 2 * LANES:
        field_v[:, LANES : width - LANES] = smooth_ref[:, LANES : width - LANES]
    field_v[:, :LANES] = jnp.where(lane < ITERS, west, smooth_ref[:, :LANES])
    field_v[:, width - LANES :] = jnp.where(lane >= LANES - ITERS, east, smooth_ref[:, width - LANES :])
    store_field = pltpu.make_async_copy(field_v, field_hbm, sem_field)
    store_field.start()

    parts = cour_ref[FIRST:].astype(jnp.bfloat16)
    for i in range(PARTS):
        columns = (per * LANES, i * per)
        source = jnp.right_shift(iota((parts.shape[1], columns[0]), 1), 7) + columns[1]
        row = iota(source.shape, 0)
        picks = (jnp.bitwise_and(row, owners - 1) == source) & (row < 3 * owners)
        spread[i] = dot(parts, picks.astype(jnp.float32).astype(jnp.bfloat16), NN)

    for i in range(PARTS):
        loads[i].wait()
        for o in range(i * per, (i + 1) * per):
            begin = (o - i * per) * LANES
            out_v[o] = grown_by(rows_v[o], spread[i, :, begin : begin + LANES])
        stores[i].start()
    store_field.wait()
    for c in stores:
        c.wait()


def finish(where, cour, smoothed, left, right, got_left, got_right, rows, onto):
    hbm = pl.BlockSpec(memory_space=pltpu.HBM)
    vm = pl.BlockSpec(memory_space=pltpu.VMEM)
    return pl.pallas_call(
        finish_kernel,
        in_specs=[pl.BlockSpec(memory_space=pltpu.SMEM)] + [vm] * 6 + [hbm] * 2,
        out_specs=(hbm, hbm),
        out_shape=(
            jax.ShapeDtypeStruct(onto.shape, jnp.float32),
            jax.ShapeDtypeStruct(smoothed.shape, jnp.float32),
        ),
        scratch_shapes=[
            pltpu.VMEM(rows.shape, jnp.float32),
            pltpu.VMEM(rows.shape, jnp.float32),
            pltpu.VMEM(smoothed.shape, jnp.float32),
            pltpu.VMEM((PARTS, rows.shape[1], rows.shape[0] // PARTS * LANES), jnp.float32),
            pltpu.SemaphoreType.DMA((PARTS,)),
            pltpu.SemaphoreType.DMA((PARTS,)),
            pltpu.SemaphoreType.DMA,
        ],
        input_output_aliases={8: 0},
        compiler_params=params(24),
        name="finish",
    )(where, cour, smoothed, left, right, got_left, got_right, rows, onto)


def neighbours(low_part, high_part, axis):
    count = lax.axis_size(axis)
    forward = [(i, i + 1) for i in range(count - 1)]
    backward = [(i + 1, i) for i in range(count - 1)]
    return lax.ppermute(high_part, axis, forward), lax.ppermute(low_part, axis, backward)


def per_device(parcels, growth_rate, cell_index, dest_owner, live_count, supersat, bin_volume):
    owners = lax.axis_size("own")
    total = parcels.shape[0]
    cap = 2 * total // owners
    chunks = total // LANES
    square = lambda x: x.reshape(chunks, LANES)
    exchange = functools.partial(lax.all_to_all, axis_name="own", split_axis=0, concat_axis=0, tiled=True)
    where = jnp.stack([lax.axis_index("grp"), lax.axis_index("own"), lax.axis_size("grp"), owners]).astype(jnp.int32)
    first, src = plan(
        live_count, square(dest_owner), square(growth_rate), square(cell_index), bin_volume.reshape(1, LANES), parcels, owners, cap
    )
    got_first = exchange(first)
    rest = pack(src, parcels)
    got_rest = exchange(rest)

    field, cour, top, bottom, left, right = deposit(got_first, supersat)
    got_up, got_down = neighbours(top, bottom, "grp")
    left, right = sides(got_up, got_down, left, right)
    got_left, got_right = neighbours(left, right, "own")
    smoothed = smooth(where, field, got_up, got_down)
    onto = grow_first(got_first, cour)
    grown, field = finish(where, cour, smoothed, left, right, got_left, got_right, got_rest, onto)
    return grown.reshape(owners * cap, LANES), field


def solution(mesh):
    placed = (
        P(("grp", "own"), None),
        P(("grp", "own")),
        P(("grp", "own")),
        P(("grp", "own")),
        P(("grp", "own")),
        P("grp", "own"),
        P(),
    )
    return jax.shard_map(
        per_device,
        mesh=mesh,
        in_specs=placed,
        out_specs=(P(("grp", "own"), None), P("grp", "own")),
        check_vma=False,
    )
```
